32 devices in a mesh: frames: 4 (over y, x), rows: 8 (over z, core).
Axes of the slice: x: 2, y: 2, z: 4, core: 2. Of those that a mesh axis runs over, the one named last changes fastest.
Arguments:
- latents: bfloat16 [8, 32, 40, 512], P('frames', 'rows'), may hold values from -100 to 100
- norm_gain: float32 [512], replicated, may hold values from 0.1 to 1.9
- norm_bias: float32 [512], replicated, may hold values from -3 to 3
- conv_weight: bfloat16 [3, 3, 3, 512, 512], P(None, None, None, None, ('frames', 'rows')), may hold values from -0.0546875 to 0.0546875
- conv_bias: float32 [512], replicated, may hold values from -3 to 3
Outputs:
- branch_out: bfloat16 [8, 32, 40, 512], P('frames', 'rows')
The draws below stay inside these ranges and needn't reach their ends.
All inputs are finite; a program needn't handle non-finite values.
Results may differ from the reference program's by a relative error of at most 0.0043.
Values may be sent and summed in bfloat16 or wider, within the bound.
No kernel may reach another device: no remote copies, remote signals or barrier semaphores. Data moves between devices by JAX's collectives and lax.ppermute only.
A program may use at most 128 MiB of HBM per device.

```python
import math
import jax
import jax.numpy as jnp
from jax import lax

C = 512
GROUPS = 32
WIDTH = 40
FRAMES = 8
HEIGHT = 32


def draw_latents(key, part):
    key_noise = jax.random.fold_in(key, 11)
    key_offset = jax.random.fold_in(key, 12)
    key_scale = jax.random.fold_in(key, 13)
    shape = (FRAMES, HEIGHT, WIDTH, C)
    row_pos = jnp.arange(HEIGHT, dtype=jnp.float32) / (HEIGHT - 1)
    frame_scale = 1.0 + 0.5 * jnp.arange(FRAMES, dtype=jnp.float32) / max(FRAMES - 1, 1)
    random_part = jax.random.normal(key_noise, shape, jnp.float32)
    row_scale = 1.0 + 2.0 * row_pos
    chan_scale = jnp.exp(jax.random.uniform(key_scale, (C,), jnp.float32, 0.0, math.log(2.0)))
    offset = 0.5 * jax.random.normal(key_offset, (C,), jnp.float32)
    values = random_part * frame_scale[:, None, None, None] * row_scale[None, :, None, None] * chan_scale + offset
    return jnp.clip(values, -100.0, 100.0).astype(jnp.bfloat16)


def steps_of(rng, shape, pieces, low, largest):
    factor_of = 1.0
    for position, shards_of in pieces:
        draws = jax.random.uniform(jax.random.fold_in(jax.random.fold_in(rng, 6), position), (shards_of,), jnp.float32, low / len(pieces), largest / len(pieces))
        factor_of = factor_of * jnp.repeat(jnp.exp(draws), shape[position] // shards_of).reshape((-1,) + (1,) * (len(shape) - 1 - position))
    return factor_of


def scatter_about(stream_key, extent, scale, limit, cuts=(), kind=jnp.bfloat16):
    values = jax.random.normal(stream_key, extent, jnp.float32) * scale
    if len(cuts) > 0:
        values = steps_of(stream_key, extent, cuts, -0.22, 0.18) * values
    return jnp.clip(values, min=-limit, max=limit).astype(kind)


def setup_inputs(seed: int = 0) -> dict:
    streams_of = jax.random.split(jax.random.key(seed), 6)
    return {
        "latents": draw_latents(jax.random.fold_in(streams_of[5], 71), 0),
        "norm_gain": jnp.clip(1.0 + 0.18 * jax.random.normal(streams_of[1], (C,), jnp.float32), 0.1, 1.9),
        "norm_bias": scatter_about(streams_of[2], (C,), 0.5, 3.0, (), jnp.float32),
        "conv_weight": scatter_about(streams_of[3], (3, 3, 3, C, C), (27 * C) ** -0.5, 0.0546875, ((4, 32),)),
        "conv_bias": scatter_about(streams_of[4], (C,), 0.5, 3.0, (), jnp.float32),
    }


epsilon = 1e-06

def reference(latents, norm_gain, norm_bias, conv_weight, conv_bias):
    values = latents.astype(jnp.float32)
    frame_count, row_count, col_count, channels = values.shape
    grouped = values.reshape(frame_count, row_count, col_count, GROUPS, channels // GROUPS)
    group_mean = lax.optimization_barrier(jnp.mean(grouped, axis=(0, 1, 2, 4), keepdims=True))
    group_var = lax.optimization_barrier(jnp.mean((grouped - group_mean) ** 2, axis=(0, 1, 2, 4), keepdims=True))
    normed = ((grouped - group_mean) * lax.rsqrt(group_var + epsilon)).reshape(frame_count, row_count, col_count, channels)
    activated = jax.nn.silu(normed * norm_gain + norm_bias).astype(jnp.bfloat16)
    padded = jnp.pad(activated, ((2, 0), (0, 0), (0, 0), (0, 0)))
    padded = jnp.pad(padded, ((0, 0), (1, 1), (1, 1), (0, 0)), mode='reflect')
    output = lax.conv_general_dilated(padded.astype(jnp.float32)[None], conv_weight.astype(jnp.float32), (1, 1, 1), 'VALID', dimension_numbers=('NDHWC', 'DHWIO', 'NDHWC'), precision=lax.Precision.HIGHEST)[0]
    return (output + conv_bias).astype(jnp.bfloat16)
```

```python
import functools

import jax
import jax.numpy as jnp
from jax import lax
from jax.experimental import pallas as pl
from jax.experimental.pallas import tpu as pltpu
from jax.sharding import PartitionSpec as P

GROUPS = 32
LANES = 128

epsilon = 1e-06

whole = pl.BlockSpec(memory_space=pltpu.VMEM)
scalars = pl.BlockSpec(memory_space=pltpu.SMEM)


def params(mib):
    return pltpu.CompilerParams(vmem_limit_bytes=mib * 2**20)


def flip(axis, distance):
    return [(i, i ^ distance) for i in range(lax.axis_size(axis))]


def stats_kernel(x_ref, out_ref):
    frames, rows, cols, channels = x_ref.shape
    entries = frames * rows * cols
    for block in range(channels // LANES):
        lanes = pl.ds(block * LANES, LANES)
        total = jnp.zeros((8, LANES), jnp.float32)
        for f in range(frames):
            for r in range(rows):
                x = x_ref[f, r, :, lanes].astype(jnp.float32)
                total = total + jnp.sum(x.reshape(-1, 8, LANES), axis=0)
        mean = jnp.sum(total, axis=0, keepdims=True) / entries
        total = jnp.zeros((8, LANES), jnp.float32)
        for f in range(frames):
            for r in range(rows):
                x = x_ref[f, r, :, lanes].astype(jnp.float32) - mean
                total = total + jnp.sum((x * x).reshape(-1, 8, LANES), axis=0)
        out_ref[0:1, lanes] = mean
        out_ref[1:2, lanes] = jnp.sum(total, axis=0, keepdims=True)


def local_stats(latents):
    return pl.pallas_call(
        stats_kernel,
        out_shape=jax.ShapeDtypeStruct((2, latents.shape[3]), jnp.float32),
        in_specs=[whole],
        out_specs=whole,
        compiler_params=params(8),
    )(latents)


def merge(one, other, entries):
    apart = one[0] - other[0]
    mean = 0.5 * (one[0] + other[0])
    return jnp.stack([mean, one[1] + other[1] + apart * apart * (0.5 * entries)])


def group_stats(stats, entries):
    channels = stats.shape[1]
    means = stats[0].reshape(GROUPS, channels // GROUPS)
    apart = stats[1].reshape(GROUPS, channels // GROUPS)
    mean = jnp.mean(means, axis=1, keepdims=True)
    spread = jnp.sum(apart + entries * (means - mean) ** 2, axis=1, keepdims=True)
    var = spread / (entries * (channels // GROUPS))
    scale = lax.rsqrt(var + epsilon)
    shape = means.shape
    return (
        jnp.broadcast_to(mean, shape).reshape(channels),
        jnp.broadcast_to(scale, shape).reshape(channels),
    )


def activate_kernel(place_ref, norm_ref, *refs):
    *piece_refs, even_ref, odd_ref, scratch = refs
    held, rows, cols, channels = piece_refs[0].shape
    frames = held * len(piece_refs)
    blocks = channels // LANES

    def step(index, carry):
        r = index // blocks
        lanes = pl.ds(pl.multiple_of((index % blocks) * LANES, LANES), LANES)
        mean = norm_ref[0:1, lanes]
        scale = norm_ref[1:2, lanes]
        bias = norm_ref[2:3, lanes]
        for p, piece_ref in enumerate(piece_refs):
            for f in range(held):
                x = piece_ref[f, r, :, lanes].astype(jnp.float32)
                v = (x - mean) * scale + bias
                h = 0.5 * v
                scratch[pl.ds(frames + place_ref[p] + f, cols, stride=frames), :] = h + h * jnp.tanh(h)
        last = (cols + 1) * frames
        scratch[0:frames, :] = scratch[2 * frames : 3 * frames, :]
        scratch[last : last + frames, :] = scratch[last - 2 * frames : last - frames, :]
        even_ref[r, :, lanes] = scratch[...].astype(jnp.bfloat16)
        odd_ref[r, :, lanes] = scratch[frames:last, :].astype(jnp.bfloat16)
        return carry

    lax.fori_loop(0, rows * blocks, step, 0)


def activate(places, norm, pieces):
    held, rows, cols, channels = pieces[0].shape
    frames = held * len(pieces)
    return pl.pallas_call(
        activate_kernel,
        out_shape=(
            jax.ShapeDtypeStruct((rows, (cols + 2) * frames, channels), jnp.bfloat16),
            jax.ShapeDtypeStruct((rows, cols * frames, channels), jnp.bfloat16),
        ),
        in_specs=[scalars, whole] + [whole] * len(pieces),
        out_specs=(whole, whole),
        scratch_shapes=[pltpu.VMEM(((cols + 2) * frames, LANES), jnp.float32)],
        compiler_params=params(24),
        cost_estimate=pl.CostEstimate(
            flops=10 * frames * rows * cols * channels,
            bytes_accessed=6 * frames * rows * cols * channels,
            transcendentals=frames * rows * cols * channels,
        ),
    )(places, norm, *pieces)


def conv_kernel(count, held, place_ref, slot_ref, even_ref, odd_ref, bias_ref, *refs):
    piece_refs, refs = refs[:count], refs[count:]
    out_refs, (taps, sums, placed) = refs[:-3], refs[-3:]
    rows = even_ref.shape[0] - 2
    per_row = odd_ref.shape[1]
    frames = held * len(out_refs)
    cols = per_row // frames
    channels = even_ref.shape[2]
    width = taps.shape[2] * taps.shape[3]
    for p, piece_ref in enumerate(piece_refs):
        slot = slot_ref[p]
        for tap in range(27):
            taps[tap % 9, tap // 9, slot] = piece_ref[tap]

    for tap in range(9):
        b, c = tap // 3, tap % 3
        weight = taps[tap].reshape(3 * width, channels)
        for y in range(rows):
            if c == 1:
                window = odd_ref[y + b]
            else:
                window = even_ref[y + b, pl.ds(c * frames, per_row), :]
            product = lax.dot_general(
                window, weight, (((1,), (1,)), ((), ())), preferred_element_type=jnp.float32
            )
            for a in range(3):
                part = product[:, a * width : (a + 1) * width]
                if tap == 0:
                    sums[a, y * per_row : (y + 1) * per_row, :] = part
                else:
                    sums[a, y * per_row : (y + 1) * per_row, :] += part

    for f in range(frames):
        value = bias_ref[...] + jnp.zeros((rows * cols, width), jnp.float32)
        for a in range(3):
            if f + a >= 2:
                value = value + sums[a, pl.ds(f + a - 2, rows * cols, stride=frames), :]
        placed[f] = value.astype(jnp.bfloat16)
    for p, out_ref in enumerate(out_refs):
        out_ref[...] = placed[pl.ds(place_ref[p], held)]


def convolve(places, slots, even, odd, bias, pieces, groups, held):
    rows, per_row, channels = even.shape[0] - 2, odd.shape[1], even.shape[2]
    frames = held * groups
    positions = rows * per_row // frames
    each = pieces[0].shape[1]
    width = each * len(pieces)
    return pl.pallas_call(
        functools.partial(conv_kernel, len(pieces), held),
        out_shape=tuple(
            jax.ShapeDtypeStruct((held, positions, width), jnp.bfloat16) for _ in range(groups)
        ),
        in_specs=[scalars, scalars] + [whole] * (3 + len(pieces)),
        out_specs=tuple(whole for _ in range(groups)),
        scratch_shapes=[
            pltpu.VMEM((9, 3, len(pieces), each, channels), jnp.bfloat16),
            pltpu.VMEM((3, rows * per_row, width), jnp.float32),
            pltpu.VMEM((frames, positions, width), jnp.bfloat16),
        ],
        compiler_params=params(32),
        cost_estimate=pl.CostEstimate(
            flops=2 * 27 * rows * per_row * channels * width,
            bytes_accessed=2 * 27 * channels * width + 4 * even.size,
            transcendentals=0,
        ),
    )(places, slots, even, odd, bias, *pieces)


def place_kernel(place_ref, *refs):
    *piece_refs, out_ref = refs
    width = piece_refs[0].shape[2]
    for p, piece_ref in enumerate(piece_refs):
        start = pl.multiple_of(place_ref[p] * width, LANES)
        out_ref[:, :, pl.ds(start, width)] = piece_ref[...]


def place(groups, pieces):
    held, positions, width = pieces[0].shape
    return pl.pallas_call(
        place_kernel,
        out_shape=jax.ShapeDtypeStruct((held, positions, width * len(pieces)), jnp.bfloat16),
        in_specs=[scalars] + [whole] * len(pieces),
        out_specs=whole,
        compiler_params=params(8),
    )(groups, *pieces)


def line_pieces(weight):
    cores = 2

    def both(pairs):
        return [(cores * a + c, cores * b + c) for a, b in pairs for c in range(cores)]

    second = lax.ppermute(weight, "rows", flip("rows", 2 * cores))
    first = lax.ppermute(weight, "rows", flip("rows", cores))
    middle, second = lax.optimization_barrier((weight, second))
    third_ends = lax.ppermute(second, "rows", both([(1, 0), (2, 3)]))
    third_middle = lax.ppermute(middle, "rows", both([(1, 2), (2, 1)]))
    chip = lax.axis_index("rows") // cores
    third = jnp.where((chip == 0) | (chip == 3), third_ends, third_middle)
    mine = [weight, first, second, third]
    return mine + [lax.ppermute(piece, "rows", flip("rows", 1)) for piece in mine]


def body(latents, norm_gain, norm_bias, conv_weight, conv_bias):
    held, row_count, col_count, channels = latents.shape
    group_count = lax.axis_size("frames")
    strips = lax.axis_size("rows")
    group = lax.axis_index("frames")
    strip = lax.axis_index("rows")

    forward = [(i, i + 1) for i in range(strips - 1)]
    backward = [(i + 1, i) for i in range(strips - 1)]
    above = lax.ppermute(latents[:, row_count - 1 :], "rows", forward)
    below = lax.ppermute(latents[:, :1], "rows", backward)

    weight = conv_weight.transpose(0, 1, 2, 4, 3)
    weight = weight.reshape((-1,) + weight.shape[3:])
    if strips == 8:
        pieces = line_pieces(weight)
        slots = jnp.stack([strip ^ (2 * d) ^ c for c in range(2) for d in range(4)])
    else:
        gathered = lax.all_gather(weight, "rows", axis=1, tiled=True)
        pieces, slots = [gathered], jnp.zeros((1,), jnp.int32)

    above = jnp.where(strip == 0, latents[:, 1:2], above)
    below = jnp.where(strip == strips - 1, latents[:, row_count - 2 : row_count - 1], below)
    rowed = jnp.concatenate([above, latents, below], axis=1)
    strip_pieces = [rowed] + [
        lax.ppermute(rowed, "frames", flip("frames", d)) for d in range(1, group_count)
    ]

    stats = local_stats(latents)
    entries = held * row_count * col_count
    for axis in ("rows", "frames"):
        distance = 1
        while distance < lax.axis_size(axis):
            stats = merge(stats, lax.ppermute(stats, axis, flip(axis, distance)), entries)
            entries *= 2
            distance *= 2
    mean, scale = group_stats(stats, entries)
    norm = jnp.stack([mean, scale * norm_gain, norm_bias])

    groups = jnp.stack([group ^ d for d in range(group_count)]).astype(jnp.int32)
    even, odd = activate(groups * held, norm, strip_pieces)

    width = channels // group_count
    bias = lax.dynamic_slice_in_dim(conv_bias, group * width, width)[None]
    parts = convolve(
        groups * held, slots.astype(jnp.int32), even, odd, bias, pieces, group_count, held
    )
    parts = [parts[0]] + [
        lax.ppermute(parts[d], "frames", flip("frames", d)) for d in range(1, group_count)
    ]
    return place(groups, parts).reshape(latents.shape)


def solution(mesh):
    placed = (
        P("frames", "rows", None, None),
        P(),
        P(),
        P(None, None, None, None, ("frames", "rows")),
        P(),
    )
    return jax.shard_map(
        body, mesh=mesh, in_specs=placed, out_specs=P("frames", "rows", None, None), check_vma=False
    )
```

```python
import functools

import jax
import jax.numpy as jnp
from jax import lax
from jax.experimental import pallas as pl
from jax.experimental.pallas import tpu as pltpu
from jax.sharding import PartitionSpec as P

GROUPS = 32
LANES = 128
CORES = 2

epsilon = 1e-06

whole = pl.BlockSpec(memory_space=pltpu.VMEM)
scalars = pl.BlockSpec(memory_space=pltpu.SMEM)


def params(mib):
    return pltpu.CompilerParams(vmem_limit_bytes=mib * 2**20)


def flip(axis, distance):
    return [(i, i ^ distance) for i in range(lax.axis_size(axis))]


def exchange(block, axis, distances):
    return [lax.ppermute(block, axis, flip(axis, d)) for d in distances]


def chip_pairs(pairs):
    return [(CORES * a + c, CORES * b + c) for a, b in pairs for c in range(CORES)]


def after(block, *others):
    return lax.optimization_barrier((block, *others))[0]


def stats_kernel(x_ref, out_ref):
    frames, rows, cols, channels = x_ref.shape
    entries = frames * rows * cols
    for block in range(channels // LANES):
        lanes = pl.ds(block * LANES, LANES)
        total = jnp.zeros((8, LANES), jnp.float32)
        for f in range(frames):
            for r in range(rows):
                x = x_ref[f, r, :, lanes].astype(jnp.float32)
                total = total + jnp.sum(x.reshape(-1, 8, LANES), axis=0)
        mean = jnp.sum(total, axis=0, keepdims=True) / entries
        total = jnp.zeros((8, LANES), jnp.float32)
        for f in range(frames):
            for r in range(rows):
                x = x_ref[f, r, :, lanes].astype(jnp.float32) - mean
                total = total + jnp.sum((x * x).reshape(-1, 8, LANES), axis=0)
        out_ref[0:1, lanes] = mean
        out_ref[1:2, lanes] = jnp.sum(total, axis=0, keepdims=True)


def local_stats(latents):
    return pl.pallas_call(
        stats_kernel,
        out_shape=jax.ShapeDtypeStruct((2, latents.shape[3]), jnp.float32),
        in_specs=[whole],
        out_specs=whole,
        compiler_params=params(8),
    )(latents)


def merge(parts, entries):
    mean = sum(part[0] for part in parts) / len(parts)
    apart = sum((part[0] - mean) ** 2 for part in parts) * entries
    return jnp.stack([mean, sum(part[1] for part in parts) + apart])


def pack_kernel(edge_ref, stats_ref, above_ref, x_ref, below_ref, out_ref):
    frames, rows, cols, _ = x_ref.shape
    count = frames * (rows + 2) * cols
    for f in range(frames):
        start = f * (rows + 2) * cols
        out_ref[start + cols : start + (rows + 1) * cols, :] = x_ref[f].reshape(rows * cols, -1)
        last = start + (rows + 1) * cols

        @pl.when(edge_ref[0] == 0)
        def _():
            out_ref[start : start + cols, :] = above_ref[f, 0]

        @pl.when(edge_ref[0] != 0)
        def _():
            out_ref[start : start + cols, :] = x_ref[f, 1]

        @pl.when(edge_ref[1] == 0)
        def _():
            out_ref[last : last + cols, :] = below_ref[f, 0]

        @pl.when(edge_ref[1] != 0)
        def _():
            out_ref[last : last + cols, :] = x_ref[f, rows - 2]

    rest = stats_ref[...]
    terms = []
    for _ in range(3):
        term = rest.astype(jnp.bfloat16).astype(jnp.float32)
        terms.append(term)
        rest = rest - term
    unused = out_ref.shape[0] - count - 6
    terms.append(jnp.zeros((unused, rest.shape[1]), jnp.float32))
    out_ref[count:, :] = jnp.concatenate(terms, axis=0).astype(jnp.bfloat16)


def pack(edges, stats, above, latents, below):
    frames, rows, cols, channels = latents.shape
    return pl.pallas_call(
        pack_kernel,
        out_shape=jax.ShapeDtypeStruct((frames * (rows + 2) * cols + 16, channels), jnp.bfloat16),
        in_specs=[scalars] + [whole] * 4,
        out_specs=whole,
        compiler_params=params(8),
    )(edges, stats, above, latents, below)


def lane_group_sum(x, size):
    lane = lax.broadcasted_iota(jnp.int32, x.shape, 1)
    step = 1
    while step < size:
        up = pltpu.roll(x, x.shape[1] - step, 1)
        down = pltpu.roll(x, step, 1)
        x = x + jnp.where((lane & step) == 0, up, down)
        step *= 2
    return x


def activate_kernel(held, rows, entries, place_ref, affine_ref, *refs):
    *piece_refs, even_ref, odd_ref, scratch = refs
    channels = piece_refs[0].shape[1]
    frames = held * len(piece_refs)
    cols = odd_ref.shape[1] // frames
    tail = held * rows * cols
    size = channels // GROUPS

    def step(index, carry):
        lanes = pl.ds(pl.multiple_of(index * LANES, LANES), LANES)
        means, squares = [], []
        for piece_ref in piece_refs:
            terms = piece_ref[tail : tail + 16, lanes].astype(jnp.float32)
            both = terms[0:2] + terms[2:4] + terms[4:6]
            means.append(both[0:1])
            squares.append(both[1:2])
        count = len(piece_refs) * size
        mean = lane_group_sum(jnp.broadcast_to(sum(means), (8, LANES)), size) / count
        spread = sum(squares) + entries * sum((m - mean[0:1]) ** 2 for m in means)
        var = lane_group_sum(jnp.broadcast_to(spread, (8, LANES)), size) / (count * entries)
        mean = mean[0:1]
        scale = lax.rsqrt(var[0:1] + epsilon) * affine_ref[0:1, lanes]
        bias = affine_ref[1:2, lanes]
        last = (cols + 1) * frames
        for r in range(rows):
            for p, piece_ref in enumerate(piece_refs):
                for f in range(held):
                    start = (f * rows + r) * cols
                    x = piece_ref[start : start + cols, lanes].astype(jnp.float32)
                    h = 0.5 * ((x - mean) * scale + bias)
                    scratch[r, pl.ds(frames + place_ref[p] + f, cols, stride=frames), :] = h + h * jnp.tanh(h)
            scratch[r, 0:frames, :] = scratch[r, 2 * frames : 3 * frames, :]
            scratch[r, last : last + frames, :] = scratch[r, last - 2 * frames : last - frames, :]
            even_ref[r, :, lanes] = scratch[r].astype(jnp.bfloat16)
            odd_ref[r, :, lanes] = scratch[r, frames:last, :].astype(jnp.bfloat16)
        return carry

    lax.fori_loop(0, channels // LANES, step, 0)


def activate(places, affine, pieces, held, rows, cols, entries):
    channels = pieces[0].shape[1]
    frames = held * len(pieces)
    return pl.pallas_call(
        functools.partial(activate_kernel, held, rows, entries),
        out_shape=(
            jax.ShapeDtypeStruct((rows, (cols + 2) * frames, channels), jnp.bfloat16),
            jax.ShapeDtypeStruct((rows, cols * frames, channels), jnp.bfloat16),
        ),
        in_specs=[scalars, whole] + [whole] * len(pieces),
        out_specs=(whole, whole),
        scratch_shapes=[pltpu.VMEM((rows, (cols + 2) * frames, LANES), jnp.float32)],
        compiler_params=params(24),
        cost_estimate=pl.CostEstimate(
            flops=10 * frames * rows * cols * channels,
            bytes_accessed=6 * frames * rows * cols * channels,
            transcendentals=frames * rows * cols * channels,
        ),
    )(places, affine, *pieces)


def conv_kernel(count, with_other, place_ref, slot_ref, half_ref, even_ref, odd_ref, bias_ref, *refs):
    piece_refs, refs = refs[:count], refs[count:]
    if with_other:
        other_ref, refs = refs[0], refs[1:]
    out_refs, (taps, sums, placed) = refs[:-3], refs[-3:]
    rows = even_ref.shape[0] - 2
    per_row = odd_ref.shape[1]
    frames = placed.shape[0]
    cols = per_row // frames
    channels = even_ref.shape[2]
    width = taps.shape[2] * taps.shape[3]
    for p, piece_ref in enumerate(piece_refs):
        slot = slot_ref[p]
        for tap in range(27):
            taps[tap % 9, tap // 9, slot] = piece_ref[tap]

    for y in range(rows):
        total = None
        for tap in range(9):
            b, c = tap // 3, tap % 3
            if c == 1:
                window = odd_ref[y + b]
            else:
                window = even_ref[y + b, pl.ds(c * frames, per_row), :]
            product = lax.dot_general(
                window,
                taps[tap].reshape(3 * width, channels),
                (((1,), (1,)), ((), ())),
                preferred_element_type=jnp.float32,
            )
            total = product if total is None else total + product
        place = slice(y * per_row, (y + 1) * per_row)
        sums[0, place, :] = total[:, : 2 * width]
        sums[1, place, 0:width] = total[:, 2 * width :]

    count = rows * cols
    lane = lax.broadcasted_iota(jnp.int32, (count, 2 * width), 1)
    low = lane < width
    for f in range(frames):
        value = sums[1, pl.ds(f, count, stride=frames), :]
        if f >= 1:
            value = value + pltpu.roll(sums[0, pl.ds(f - 1, count, stride=frames), :], width, 1)
        if f >= 2:
            value = value + sums[0, pl.ds(f - 2, count, stride=frames), :]
        value = jnp.where(low, value, pltpu.roll(value, width, 1)) + bias_ref[...]
        if with_other:
            value = jnp.where(low == (half_ref[0] == 0), value, other_ref[f].astype(jnp.float32))
        placed[f] = value.astype(jnp.bfloat16)
    if with_other:
        for p, out_ref in enumerate(out_refs):
            out_ref[...] = placed[pl.ds(place_ref[p], out_ref.shape[0])]
    else:
        out_refs[0][...] = placed[...]


def convolve(places, slots, half, even, odd, bias, pieces, frames, other=None):
    rows, per_row, channels = even.shape[0] - 2, odd.shape[1], even.shape[2]
    positions = rows * per_row // frames
    each = pieces[0].shape[1]
    width = each * len(pieces)
    if other is None:
        shapes, others = [(frames, positions, 2 * width)], []
    else:
        groups = places.shape[0]
        shapes, others = [(frames // groups, positions, 2 * width)] * groups, [other]
    return pl.pallas_call(
        functools.partial(conv_kernel, len(pieces), other is not None),
        out_shape=tuple(jax.ShapeDtypeStruct(shape, jnp.bfloat16) for shape in shapes),
        in_specs=[scalars] * 3 + [whole] * (3 + len(pieces) + len(others)),
        out_specs=tuple(whole for _ in shapes),
        scratch_shapes=[
            pltpu.VMEM((9, 3, len(pieces), each, channels), jnp.bfloat16),
            pltpu.VMEM((2, rows * per_row, 2 * width), jnp.float32),
            pltpu.VMEM((frames, positions, 2 * width), jnp.bfloat16),
        ],
        compiler_params=params(32),
        cost_estimate=pl.CostEstimate(
            flops=2 * rows * per_row * channels * width,
            bytes_accessed=2 * channels * width,
            transcendentals=0,
        ),
    )(places, slots, half, even, odd, bias, *pieces, *others)


def place_kernel(place_ref, *refs):
    *piece_refs, out_ref = refs
    width = piece_refs[0].shape[2]
    for p, piece_ref in enumerate(piece_refs):
        start = pl.multiple_of(place_ref[p] * width, LANES)
        out_ref[:, :, pl.ds(start, width)] = piece_ref[...]


def place(groups, pieces):
    held, positions, width = pieces[0].shape
    return pl.pallas_call(
        place_kernel,
        out_shape=jax.ShapeDtypeStruct((held, positions, width * len(pieces)), jnp.bfloat16),
        in_specs=[scalars] + [whole] * len(pieces),
        out_specs=whole,
        compiler_params=params(8),
    )(groups, *pieces)


def body(latents, norm_gain, norm_bias, conv_weight, conv_bias):
    held, row_count, col_count, channels = latents.shape
    group_count = lax.axis_size("frames")
    strips = lax.axis_size("rows")
    group = lax.axis_index("frames")
    strip = lax.axis_index("rows")
    is_line = strips == 4 * CORES
    weight = conv_weight.transpose(0, 1, 2, 4, 3)
    weight = weight.reshape((-1,) + weight.shape[3:])

    above = lax.ppermute(latents[:, row_count - 1 :], "rows", [(i, i + 1) for i in range(strips - 1)])
    below = lax.ppermute(latents[:, :1], "rows", [(i + 1, i) for i in range(strips - 1)])

    entries = held * row_count * col_count
    stats = local_stats(latents)
    if is_line:
        stats = merge([stats] + exchange(stats, "rows", [1]), entries)
        chips = range(CORES, strips, CORES)
        stats = merge([stats] + exchange(stats, "rows", chips), CORES * entries)
        entries *= strips
    else:
        distance = 1
        while distance < strips:
            stats = merge([stats] + exchange(stats, "rows", [distance]), entries)
            entries *= 2
            distance *= 2

    if is_line:
        weight = after(weight, stats, above, below)
        first, second = exchange(weight, "rows", [CORES, 2 * CORES])
        weight, first, second = lax.optimization_barrier((weight, first, second))
        ends = chip_pairs([(1, 0), (2, 3)])
        middle = chip_pairs([(1, 2), (2, 1)])
        third_ends = lax.ppermute(second, "rows", ends)
        third_middle = lax.ppermute(weight, "rows", middle)

    edges = jnp.stack([strip == 0, strip == strips - 1]).astype(jnp.int32)
    payload = pack(edges, stats, above, latents, below)
    strip_pieces = [payload] + exchange(payload, "frames", range(1, group_count))
    groups = jnp.stack([group ^ d for d in range(group_count)]).astype(jnp.int32)
    affine = jnp.stack([norm_gain, norm_bias])
    if is_line:
        near, strip_pieces, far = lax.optimization_barrier(([weight, first], strip_pieces, [second]))
    even, odd = activate(
        groups * held, affine, strip_pieces, held, row_count + 2, col_count, entries
    )

    width = channels // group_count
    bias = lax.dynamic_slice_in_dim(conv_bias, group * width, width)[None]
    if is_line:
        near += [lax.ppermute(piece, "rows", flip("rows", 1)) for piece in near]
        slots = jnp.stack([strip, strip ^ 2, strip ^ 1, strip ^ 3]) % 4
        half, other_half = (strip // 4)[None], 1 - (strip // 4)[None]
    else:
        gathered = lax.all_gather(weight, "rows", axis=1, tiled=True)
        near, far = [gathered[:, : width // 2]], [gathered[:, width // 2 :]]
        slots = jnp.zeros((1,), jnp.int32)
        half, other_half = slots, slots + 1
    convolved = functools.partial(
        convolve, groups * held, slots, even=even, odd=odd, bias=bias, frames=held * group_count
    )
    done = convolved(half, pieces=near)[0]
    if is_line:
        third_ends, third_middle, done = lax.optimization_barrier((third_ends, third_middle, done))
        chip = strip // CORES
        third = jnp.where((chip == 0) | (chip == 3), third_ends, third_middle)
        far.append(third)
        far += [lax.ppermute(piece, "rows", flip("rows", 1)) for piece in far]
    parts = convolved(other_half, pieces=far, other=done)
    parts = [parts[0]] + [
        lax.ppermute(parts[d], "frames", flip("frames", d)) for d in range(1, group_count)
    ]
    return place(groups, parts).reshape(latents.shape)


def solution(mesh):
    placed = (
        P("frames", "rows", None, None),
        P(),
        P(),
        P(None, None, None, None, ("frames", "rows")),
        P(),
    )
    return jax.shard_map(
        body, mesh=mesh, in_specs=placed, out_specs=P("frames", "rows", None, None), check_vma=False
    )
```

```python
import functools

import jax
import jax.numpy as jnp
from jax import lax
from jax.experimental import pallas as pl
from jax.experimental.pallas import tpu as pltpu
from jax.sharding import PartitionSpec as P

GROUPS = 32
LANES = 128
CORES = 2

epsilon = 1e-06

whole = pl.BlockSpec(memory_space=pltpu.VMEM)
scalars = pl.BlockSpec(memory_space=pltpu.SMEM)


def params(mib):
    return pltpu.CompilerParams(vmem_limit_bytes=mib * 2**20)


def flip(axis, distance):
    return [(i, i ^ distance) for i in range(lax.axis_size(axis))]


def exchange(block, axis, distances):
    return [lax.ppermute(block, axis, flip(axis, d)) for d in distances]


def chip_pairs(pairs):
    return [(CORES * a + c, CORES * b + c) for a, b in pairs for c in range(CORES)]


def after(block, *others):
    return lax.optimization_barrier((block, *others))[0]


def local_kernel(x_ref, stats_ref, top_ref, bottom_ref, payload_ref):
    frames, rows, cols, channels = x_ref.shape
    entries = frames * rows * cols
    top_ref[...] = x_ref[:, 0:1]
    bottom_ref[...] = x_ref[:, rows - 1 : rows]
    for f in range(frames):
        start = (f * (rows + 2) + 1) * cols
        payload_ref[start : start + rows * cols, :] = x_ref[f].reshape(rows * cols, channels)
    for block in range(channels // LANES):
        lanes = pl.ds(block * LANES, LANES)
        total = jnp.zeros((8, LANES), jnp.float32)
        for f in range(frames):
            for r in range(rows):
                x = x_ref[f, r, :, lanes].astype(jnp.float32)
                total = total + jnp.sum(x.reshape(-1, 8, LANES), axis=0)
        mean = jnp.sum(total, axis=0, keepdims=True) / entries
        total = jnp.zeros((8, LANES), jnp.float32)
        for f in range(frames):
            for r in range(rows):
                x = x_ref[f, r, :, lanes].astype(jnp.float32) - mean
                total = total + jnp.sum((x * x).reshape(-1, 8, LANES), axis=0)
        stats_ref[0:1, lanes] = mean
        stats_ref[1:2, lanes] = jnp.sum(total, axis=0, keepdims=True)


def local(latents):
    frames, rows, cols, channels = latents.shape
    edge = jax.ShapeDtypeStruct((frames, 1, cols, channels), jnp.bfloat16)
    return pl.pallas_call(
        local_kernel,
        out_shape=(
            jax.ShapeDtypeStruct((2, channels), jnp.float32),
            edge,
            edge,
            jax.ShapeDtypeStruct((frames * (rows + 2) * cols + 16, channels), jnp.bfloat16),
        ),
        in_specs=[whole],
        out_specs=(whole,) * 4,
        compiler_params=params(8),
    )(latents)


def merge(parts, entries):
    mean = sum(part[0] for part in parts) / len(parts)
    apart = sum((part[0] - mean) ** 2 for part in parts) * entries
    return jnp.stack([mean, sum(part[1] for part in parts) + apart])


def pack_kernel(frames, rows, cols, edge_ref, stats_ref, above_ref, below_ref, _, out_ref):
    count = frames * rows * cols
    for f in range(frames):
        first = f * rows * cols
        last = first + (rows - 1) * cols
        for start, rim_ref, edge, mirror in (
            (first, above_ref, 0, first + 2 * cols),
            (last, below_ref, 1, last - 2 * cols),
        ):

            @pl.when(edge_ref[edge] == 0)
            def _():
                out_ref[start : start + cols, :] = rim_ref[f, 0]

            @pl.when(edge_ref[edge] != 0)
            def _():
                out_ref[start : start + cols, :] = out_ref[mirror : mirror + cols, :]

    rest = stats_ref[...]
    terms = []
    for _ in range(3):
        term = rest.astype(jnp.bfloat16).astype(jnp.float32)
        terms.append(term)
        rest = rest - term
    unused = out_ref.shape[0] - count - 6
    terms.append(jnp.zeros((unused, rest.shape[1]), jnp.float32))
    out_ref[count:, :] = jnp.concatenate(terms, axis=0).astype(jnp.bfloat16)


def pack(edges, stats, above, below, payload, frames, rows, cols):
    return pl.pallas_call(
        functools.partial(pack_kernel, frames, rows, cols),
        out_shape=jax.ShapeDtypeStruct(payload.shape, jnp.bfloat16),
        in_specs=[scalars] + [whole] * 4,
        out_specs=whole,
        input_output_aliases={4: 0},
        compiler_params=params(8),
    )(edges, stats, above, below, payload)


def held_kernel(in_ref, out_ref):
    pass


def hold(block):
    return pl.pallas_call(
        held_kernel,
        out_shape=jax.ShapeDtypeStruct(block.shape, block.dtype),
        in_specs=[pl.BlockSpec(memory_space=pl.ANY)],
        out_specs=pl.BlockSpec(memory_space=pl.ANY),
        input_output_aliases={0: 0},
        cost_estimate=pl.CostEstimate(flops=10**10, bytes_accessed=0, transcendentals=0),
    )(block)


def pick_kernel(which_ref, one_ref, other_ref, out_ref):
    @pl.when(which_ref[0] != 0)
    def _():
        out_ref[...] = one_ref[...]

    @pl.when(which_ref[0] == 0)
    def _():
        out_ref[...] = other_ref[...]


def pick(which, one, other):
    return pl.pallas_call(
        pick_kernel,
        out_shape=jax.ShapeDtypeStruct(one.shape, one.dtype),
        in_specs=[scalars] + [whole] * 2,
        out_specs=whole,
        compiler_params=params(8),
        cost_estimate=pl.CostEstimate(flops=10**10, bytes_accessed=one.size, transcendentals=0),
    )(which, one, other)


def lane_group_sum(x, size):
    lane = lax.broadcasted_iota(jnp.int32, x.shape, 1)
    step = 1
    while step < size:
        up = pltpu.roll(x, x.shape[1] - step, 1)
        down = pltpu.roll(x, step, 1)
        x = x + jnp.where((lane & step) == 0, up, down)
        step *= 2
    return x


def activate_kernel(held, rows, entries, place_ref, affine_ref, *refs):
    *piece_refs, even_ref, odd_ref, scratch, norm = refs
    channels = piece_refs[0].shape[1]
    frames = held * len(piece_refs)
    cols = odd_ref.shape[1] // frames
    tail = held * rows * cols
    size = channels // GROUPS

    def norms(lanes):
        means, squares = [], []
        for piece_ref in piece_refs:
            terms = piece_ref[tail : tail + 16, lanes].astype(jnp.float32)
            both = terms[0:2] + terms[2:4] + terms[4:6]
            means.append(both[0:1])
            squares.append(both[1:2])
        count = len(piece_refs) * size
        mean = lane_group_sum(jnp.broadcast_to(sum(means), (8, LANES)), size) / count
        spread = sum(squares) + entries * sum((m - mean[0:1]) ** 2 for m in means)
        var = lane_group_sum(jnp.broadcast_to(spread, (8, LANES)), size) / (count * entries)
        norm[0:1, lanes] = mean[0:1]
        norm[1:2, lanes] = lax.rsqrt(var[0:1] + epsilon) * affine_ref[0:1, lanes]
        norm[2:3, lanes] = affine_ref[1:2, lanes]

    blocks = channels // LANES
    for block in range(blocks):
        norms(pl.ds(block * LANES, LANES))
    last = (cols + 1) * frames

    def step(index, carry):
        pair, block = index // blocks, index % blocks
        lanes = pl.ds(pl.multiple_of(block * LANES, LANES), LANES)
        mean, scale, bias = norm[0:1, lanes], norm[1:2, lanes], norm[2:3, lanes]
        for p, piece_ref in enumerate(piece_refs):
            for f in range(held):
                start = pl.multiple_of((f * rows + 2 * pair) * cols, 16)
                x = piece_ref[pl.ds(start, 2 * cols), lanes].astype(jnp.float32)
                h = 0.5 * ((x - mean) * scale + bias)
                h = h + h * jnp.tanh(h)
                for r in range(2):
                    scratch[r, pl.ds(frames + place_ref[p] + f, cols, stride=frames), :] = h[r * cols : (r + 1) * cols]
        for r in range(2):
            scratch[r, 0:frames, :] = scratch[r, 2 * frames : 3 * frames, :]
            scratch[r, last : last + frames, :] = scratch[r, last - 2 * frames : last - frames, :]
            even_ref[2 * pair + r, :, lanes] = scratch[r].astype(jnp.bfloat16)
            odd_ref[2 * pair + r, :, lanes] = scratch[r, frames:last, :].astype(jnp.bfloat16)
        return carry

    lax.fori_loop(0, rows // 2 * blocks, step, 0)


def activate(places, affine, pieces, held, rows, cols, entries):
    channels = pieces[0].shape[1]
    frames = held * len(pieces)
    return pl.pallas_call(
        functools.partial(activate_kernel, held, rows, entries),
        out_shape=(
            jax.ShapeDtypeStruct((rows, (cols + 2) * frames, channels), jnp.bfloat16),
            jax.ShapeDtypeStruct((rows, cols * frames, channels), jnp.bfloat16),
        ),
        in_specs=[scalars, whole] + [whole] * len(pieces),
        out_specs=(whole, whole),
        scratch_shapes=[
            pltpu.VMEM((2, (cols + 2) * frames, LANES), jnp.float32),
            pltpu.VMEM((3, channels), jnp.float32),
        ],
        compiler_params=params(24),
        cost_estimate=pl.CostEstimate(
            flops=10 * frames * rows * cols * channels,
            bytes_accessed=6 * frames * rows * cols * channels,
            transcendentals=frames * rows * cols * channels,
        ),
    )(places, affine, *pieces)


def conv_kernel(count, with_other, place_ref, slot_ref, half_ref, even_ref, odd_ref, bias_ref, *refs):
    piece_refs, refs = refs[:count], refs[count:]
    if with_other:
        other_ref, refs = refs[0], refs[1:]
    out_refs, (taps, sums, placed) = refs[:-3], refs[-3:]
    rows = even_ref.shape[0] - 2
    per_row = odd_ref.shape[1]
    frames = placed.shape[0]
    cols = per_row // frames
    channels = even_ref.shape[2]
    width = taps.shape[2] * taps.shape[3]
    for p, piece_ref in enumerate(piece_refs):
        slot = slot_ref[p]
        for tap in range(27):
            taps[tap % 9, tap // 9, slot] = piece_ref[tap]

    for y in range(rows):
        total = None
        for tap in range(9):
            b, c = tap // 3, tap % 3
            if c == 1:
                window = odd_ref[y + b]
            else:
                window = even_ref[y + b, pl.ds(c * frames, per_row), :]
            product = lax.dot_general(
                window,
                taps[tap].reshape(3 * width, channels),
                (((1,), (1,)), ((), ())),
                preferred_element_type=jnp.float32,
            )
            total = product if total is None else total + product
        place = slice(y * per_row, (y + 1) * per_row)
        sums[0, place, :] = total[:, : 2 * width]
        sums[1, place, 0:width] = total[:, 2 * width :]

    count = rows * cols
    lane = lax.broadcasted_iota(jnp.int32, (count, 2 * width), 1)
    low = lane < width
    for f in range(frames):
        value = sums[1, pl.ds(f, count, stride=frames), :]
        if f >= 1:
            value = value + pltpu.roll(sums[0, pl.ds(f - 1, count, stride=frames), :], width, 1)
        if f >= 2:
            value = value + sums[0, pl.ds(f - 2, count, stride=frames), :]
        value = jnp.where(low, value, pltpu.roll(value, width, 1)) + bias_ref[...]
        if with_other:
            value = jnp.where(low == (half_ref[0] == 0), value, other_ref[f].astype(jnp.float32))
        placed[f] = value.astype(jnp.bfloat16)
    if with_other:
        for p, out_ref in enumerate(out_refs):
            out_ref[...] = placed[pl.ds(place_ref[p], out_ref.shape[0])]
    else:
        out_refs[0][...] = placed[...]


def convolve(places, slots, half, even, odd, bias, pieces, frames, other=None):
    rows, per_row, channels = even.shape[0] - 2, odd.shape[1], even.shape[2]
    positions = rows * per_row // frames
    each = pieces[0].shape[1]
    width = each * len(pieces)
    if other is None:
        shapes, others = [(frames, positions, 2 * width)], []
    else:
        groups = places.shape[0]
        shapes, others = [(frames // groups, positions, 2 * width)] * groups, [other]
    return pl.pallas_call(
        functools.partial(conv_kernel, len(pieces), other is not None),
        out_shape=tuple(jax.ShapeDtypeStruct(shape, jnp.bfloat16) for shape in shapes),
        in_specs=[scalars] * 3 + [whole] * (3 + len(pieces) + len(others)),
        out_specs=tuple(whole for _ in shapes),
        scratch_shapes=[
            pltpu.VMEM((9, 3, len(pieces), each, channels), jnp.bfloat16),
            pltpu.VMEM((2, rows * per_row, 2 * width), jnp.float32),
            pltpu.VMEM((frames, positions, 2 * width), jnp.bfloat16),
        ],
        compiler_params=params(32),
        cost_estimate=pl.CostEstimate(
            flops=2 * rows * per_row * channels * width,
            bytes_accessed=2 * channels * width,
            transcendentals=0,
        ),
    )(places, slots, half, even, odd, bias, *pieces, *others)


def place_kernel(place_ref, *refs):
    *piece_refs, out_ref = refs
    width = piece_refs[0].shape[2]
    for p, piece_ref in enumerate(piece_refs):
        start = pl.multiple_of(place_ref[p] * width, LANES)
        out_ref[:, :, pl.ds(start, width)] = piece_ref[...]


def place(groups, pieces):
    held, positions, width = pieces[0].shape
    return pl.pallas_call(
        place_kernel,
        out_shape=jax.ShapeDtypeStruct((held, positions, width * len(pieces)), jnp.bfloat16),
        in_specs=[scalars] + [whole] * len(pieces),
        out_specs=whole,
        compiler_params=params(8),
    )(groups, *pieces)


def body(latents, norm_gain, norm_bias, conv_weight, conv_bias):
    held, row_count, col_count, channels = latents.shape
    group_count = lax.axis_size("frames")
    strips = lax.axis_size("rows")
    group = lax.axis_index("frames")
    strip = lax.axis_index("rows")
    is_line = strips == 4 * CORES
    weight = conv_weight.transpose(0, 1, 2, 4, 3)
    weight = weight.reshape((-1,) + weight.shape[3:])

    stats, top, bottom, payload = local(latents)
    above = lax.ppermute(bottom, "rows", [(i, i + 1) for i in range(strips - 1)])
    below = lax.ppermute(top, "rows", [(i + 1, i) for i in range(strips - 1)])

    entries = held * row_count * col_count
    if is_line:
        chips = range(CORES, strips, CORES)
        stats = merge([stats] + exchange(stats, "rows", chips), entries)
        weight = after(weight, stats, above, below)
        first, second = exchange(weight, "rows", [CORES, 2 * CORES])
        stats = merge([stats] + exchange(stats, "rows", [1]), 4 * entries)
        entries *= strips
    else:
        distance = 1
        while distance < strips:
            stats = merge([stats] + exchange(stats, "rows", [distance]), entries)
            entries *= 2
            distance *= 2

    if is_line:
        weight, first, second = lax.optimization_barrier((weight, first, second))
        second = hold(second)
        ends = chip_pairs([(1, 0), (2, 3)])
        middle = chip_pairs([(1, 2), (2, 1)])
        third_ends = lax.ppermute(second, "rows", ends)
        third_middle = lax.ppermute(weight, "rows", middle)

    edges = jnp.stack([strip == 0, strip == strips - 1]).astype(jnp.int32)
    payload = pack(edges, stats, above, below, payload, held, row_count + 2, col_count)
    strip_pieces = [payload] + exchange(payload, "frames", range(1, group_count))
    groups = jnp.stack([group ^ d for d in range(group_count)]).astype(jnp.int32)
    affine = jnp.stack([norm_gain, norm_bias])
    if is_line:
        near, strip_pieces, far = lax.optimization_barrier(([weight, first], strip_pieces, [second]))
    even, odd = activate(
        groups * held, affine, strip_pieces, held, row_count + 2, col_count, entries
    )

    width = channels // group_count
    bias = lax.dynamic_slice_in_dim(conv_bias, group * width, width)[None]
    if is_line:
        near += [lax.ppermute(piece, "rows", flip("rows", 1)) for piece in near]
        slots = jnp.stack([strip, strip ^ 2, strip ^ 1, strip ^ 3]) % 4
        half, other_half = (strip // 4)[None], 1 - (strip // 4)[None]
    else:
        gathered = lax.all_gather(weight, "rows", axis=1, tiled=True)
        near, far = [gathered[:, : width // 2]], [gathered[:, width // 2 :]]
        slots = jnp.zeros((1,), jnp.int32)
        half, other_half = slots, slots + 1
    convolved = functools.partial(
        convolve, groups * held, slots, even=even, odd=odd, bias=bias, frames=held * group_count
    )
    done = convolved(half, pieces=near)[0]
    if is_line:
        third_ends, third_middle, done = lax.optimization_barrier((third_ends, third_middle, done))
        chip = strip // CORES
        at_end = ((chip == 0) | (chip == 3)).astype(jnp.int32)[None]
        third = pick(at_end, third_ends, third_middle)
        far.append(third)
        far += [lax.ppermute(piece, "rows", flip("rows", 1)) for piece in far]
    parts = convolved(other_half, pieces=far, other=done)
    parts = [parts[0]] + [
        lax.ppermute(parts[d], "frames", flip("frames", d)) for d in range(1, group_count)
    ]
    return place(groups, parts).reshape(latents.shape)


def solution(mesh):
    placed = (
        P("frames", "rows", None, None),
        P(),
        P(),
        P(None, None, None, None, ("frames", "rows")),
        P(),
    )
    return jax.shard_map(
        body, mesh=mesh, in_specs=placed, out_specs=P("frames", "rows", None, None), check_vma=False
    )
```

```python
import functools

import jax
import jax.numpy as jnp
from jax import lax
from jax.experimental import pallas as pl
from jax.experimental.pallas import tpu as pltpu
from jax.sharding import PartitionSpec as P

GROUPS = 32
LANES = 128
CORES = 2

epsilon = 1e-06

whole = pl.BlockSpec(memory_space=pltpu.VMEM)
scalars = pl.BlockSpec(memory_space=pltpu.SMEM)


def params(mib):
    return pltpu.CompilerParams(vmem_limit_bytes=mib * 2**20)


def flip(axis, distance):
    return [(i, i ^ distance) for i in range(lax.axis_size(axis))]


def exchange(block, axis, distances):
    return [lax.ppermute(block, axis, flip(axis, d)) for d in distances]


def chip_pairs(pairs):
    return [(CORES * a + c, CORES * b + c) for a, b in pairs for c in range(CORES)]


def after(block, *others):
    return lax.optimization_barrier((block, *others))[0]


def local_kernel(x_ref, stats_ref, top_ref, bottom_ref, payload_ref):
    frames, rows, cols, channels = x_ref.shape
    entries = frames * rows * cols
    top_ref[...] = x_ref[:, 0:1]
    bottom_ref[...] = x_ref[:, rows - 1 : rows]
    for f in range(frames):
        start = (f * (rows + 2) + 1) * cols
        payload_ref[start : start + rows * cols, :] = x_ref[f].reshape(rows * cols, channels)
    for block in range(channels // LANES):
        lanes = pl.ds(block * LANES, LANES)
        total = jnp.zeros((8, LANES), jnp.float32)
        for f in range(frames):
            for r in range(rows):
                x = x_ref[f, r, :, lanes].astype(jnp.float32)
                total = total + jnp.sum(x.reshape(-1, 8, LANES), axis=0)
        mean = jnp.sum(total, axis=0, keepdims=True) / entries
        total = jnp.zeros((8, LANES), jnp.float32)
        for f in range(frames):
            for r in range(rows):
                x = x_ref[f, r, :, lanes].astype(jnp.float32) - mean
                total = total + jnp.sum((x * x).reshape(-1, 8, LANES), axis=0)
        stats_ref[0:1, lanes] = mean
        stats_ref[1:2, lanes] = jnp.sum(total, axis=0, keepdims=True)


def local(latents):
    frames, rows, cols, channels = latents.shape
    edge = jax.ShapeDtypeStruct((frames, 1, cols, channels), jnp.bfloat16)
    return pl.pallas_call(
        local_kernel,
        out_shape=(
            jax.ShapeDtypeStruct((2, channels), jnp.float32),
            edge,
            edge,
            jax.ShapeDtypeStruct((frames * (rows + 2) * cols, channels), jnp.bfloat16),
        ),
        in_specs=[whole],
        out_specs=(whole,) * 4,
        compiler_params=params(8),
    )(latents)


def merge(parts, entries):
    mean = sum(part[0] for part in parts) / len(parts)
    apart = sum((part[0] - mean) ** 2 for part in parts) * entries
    return jnp.stack([mean, sum(part[1] for part in parts) + apart])


def pack_kernel(frames, rows, cols, edge_ref, above_ref, below_ref, _, out_ref):
    for f in range(frames):
        first = f * rows * cols
        last = first + (rows - 1) * cols
        for start, rim_ref, edge, mirror in (
            (first, above_ref, 0, first + 2 * cols),
            (last, below_ref, 1, last - 2 * cols),
        ):

            @pl.when(edge_ref[edge] == 0)
            def _():
                out_ref[start : start + cols, :] = rim_ref[f, 0]

            @pl.when(edge_ref[edge] != 0)
            def _():
                out_ref[start : start + cols, :] = out_ref[mirror : mirror + cols, :]


def pack(edges, above, below, payload, frames, rows, cols):
    return pl.pallas_call(
        functools.partial(pack_kernel, frames, rows, cols),
        out_shape=jax.ShapeDtypeStruct(payload.shape, jnp.bfloat16),
        in_specs=[scalars] + [whole] * 3,
        out_specs=whole,
        input_output_aliases={3: 0},
        compiler_params=params(8),
    )(edges, above, below, payload)


def held_kernel(in_ref, out_ref):
    pass


def hold(block):
    return pl.pallas_call(
        held_kernel,
        out_shape=jax.ShapeDtypeStruct(block.shape, block.dtype),
        in_specs=[pl.BlockSpec(memory_space=pl.ANY)],
        out_specs=pl.BlockSpec(memory_space=pl.ANY),
        input_output_aliases={0: 0},
        cost_estimate=pl.CostEstimate(flops=10**10, bytes_accessed=0, transcendentals=0),
    )(block)


def pick_kernel(which_ref, one_ref, other_ref, out_ref):
    @pl.when(which_ref[0] != 0)
    def _():
        out_ref[...] = one_ref[...]

    @pl.when(which_ref[0] == 0)
    def _():
        out_ref[...] = other_ref[...]


def pick(which, one, other):
    return pl.pallas_call(
        pick_kernel,
        out_shape=jax.ShapeDtypeStruct(one.shape, one.dtype),
        in_specs=[scalars] + [whole] * 2,
        out_specs=whole,
        compiler_params=params(8),
        cost_estimate=pl.CostEstimate(flops=10**10, bytes_accessed=one.size, transcendentals=0),
    )(which, one, other)


def lane_group_sum(x, size):
    lane = lax.broadcasted_iota(jnp.int32, x.shape, 1)
    step = 1
    while step < size:
        up = pltpu.roll(x, x.shape[1] - step, 1)
        down = pltpu.roll(x, step, 1)
        x = x + jnp.where((lane & step) == 0, up, down)
        step *= 2
    return x


def activate_kernel(origins, rows, cols, entries, place_ref, stats_ref, affine_ref, *refs):
    *piece_refs, even_ref, odd_ref, scratch, norm = refs
    channels = piece_refs[0].shape[1]
    frames = odd_ref.shape[1] // cols
    size = channels // GROUPS

    def norms(lanes):
        means = stats_ref[0:1, lanes]
        mean = lane_group_sum(jnp.broadcast_to(means, (8, LANES)), size) / size
        spread = stats_ref[1:2, lanes] + entries * (means - mean[0:1]) ** 2
        var = lane_group_sum(jnp.broadcast_to(spread, (8, LANES)), size) / (size * entries)
        norm[0:1, lanes] = mean[0:1]
        norm[1:2, lanes] = lax.rsqrt(var[0:1] + epsilon) * affine_ref[0:1, lanes]
        norm[2:3, lanes] = affine_ref[1:2, lanes]

    blocks = channels // LANES
    for block in range(blocks):
        norms(pl.ds(block * LANES, LANES))
    last = (cols + 1) * frames

    def step(index, carry):
        pair, block = index // blocks, index % blocks
        lanes = pl.ds(pl.multiple_of(block * LANES, LANES), LANES)
        mean, scale, bias = norm[0:1, lanes], norm[1:2, lanes], norm[2:3, lanes]
        for (p, shift), piece_ref in zip(origins, piece_refs):
            for f in range(piece_ref.shape[0] // (rows * cols)):
                start = pl.multiple_of((f * rows + 2 * pair) * cols, 16)
                x = piece_ref[pl.ds(start, 2 * cols), lanes].astype(jnp.float32)
                h = 0.5 * ((x - mean) * scale + bias)
                h = h + h * jnp.tanh(h)
                for r in range(2):
                    scratch[r, pl.ds(frames + place_ref[p] + shift + f, cols, stride=frames), :] = h[r * cols : (r + 1) * cols]
        for r in range(2):
            scratch[r, 0:frames, :] = scratch[r, 2 * frames : 3 * frames, :]
            scratch[r, last : last + frames, :] = scratch[r, last - 2 * frames : last - frames, :]
            even_ref[2 * pair + r, :, lanes] = scratch[r].astype(jnp.bfloat16)
            odd_ref[2 * pair + r, :, lanes] = scratch[r, frames:last, :].astype(jnp.bfloat16)
        return carry

    lax.fori_loop(0, rows // 2 * blocks, step, 0)


def activate(places, stats, affine, pieces, origins, rows, cols, entries):
    channels = pieces[0].shape[1]
    frames = sum(piece.shape[0] for piece in pieces) // (rows * cols)
    return pl.pallas_call(
        functools.partial(activate_kernel, origins, rows, cols, entries),
        out_shape=(
            jax.ShapeDtypeStruct((rows, (cols + 2) * frames, channels), jnp.bfloat16),
            jax.ShapeDtypeStruct((rows, cols * frames, channels), jnp.bfloat16),
        ),
        in_specs=[scalars, whole, whole] + [whole] * len(pieces),
        out_specs=(whole, whole),
        scratch_shapes=[
            pltpu.VMEM((2, (cols + 2) * frames, LANES), jnp.float32),
            pltpu.VMEM((3, channels), jnp.float32),
        ],
        compiler_params=params(24),
        cost_estimate=pl.CostEstimate(
            flops=10 * frames * rows * cols * channels,
            bytes_accessed=6 * frames * rows * cols * channels,
            transcendentals=frames * rows * cols * channels,
        ),
    )(places, stats, affine, *pieces)


def conv_kernel(count, with_other, place_ref, slot_ref, half_ref, even_ref, odd_ref, bias_ref, *refs):
    piece_refs, refs = refs[:count], refs[count:]
    if with_other:
        other_ref, refs = refs[0], refs[1:]
    out_refs, (taps, sums, placed) = refs[:-3], refs[-3:]
    rows = even_ref.shape[0] - 2
    per_row = odd_ref.shape[1]
    frames = placed.shape[0]
    cols = per_row // frames
    channels = even_ref.shape[2]
    width = taps.shape[2] * taps.shape[3]
    for p, piece_ref in enumerate(piece_refs):
        slot = slot_ref[p]
        for tap in range(27):
            taps[tap % 9, tap // 9, slot] = piece_ref[tap]

    for y in range(rows):
        total = None
        for tap in range(9):
            b, c = tap // 3, tap % 3
            if c == 1:
                window = odd_ref[y + b]
            else:
                window = even_ref[y + b, pl.ds(c * frames, per_row), :]
            product = lax.dot_general(
                window,
                taps[tap].reshape(3 * width, channels),
                (((1,), (1,)), ((), ())),
                preferred_element_type=jnp.float32,
            )
            total = product if total is None else total + product
        place = slice(y * per_row, (y + 1) * per_row)
        sums[0, place, :] = total[:, : 2 * width]
        sums[1, place, 0:width] = total[:, 2 * width :]

    count = rows * cols
    lane = lax.broadcasted_iota(jnp.int32, (count, 2 * width), 1)
    low = lane < width
    quarter = lane // (width // 2)
    turned = (half_ref[1] != 0) & ((quarter == 1) | (quarter == 2))
    mine = jnp.where(half_ref[1] != 0, quarter % 2, quarter // 2) == half_ref[0]
    for f in range(frames):
        value = sums[1, pl.ds(f, count, stride=frames), :]
        if f >= 1:
            value = value + pltpu.roll(sums[0, pl.ds(f - 1, count, stride=frames), :], width, 1)
        if f >= 2:
            value = value + sums[0, pl.ds(f - 2, count, stride=frames), :]
        value = jnp.where(low, value, pltpu.roll(value, width, 1))
        value = jnp.where(turned, pltpu.roll(value, width // 2, 1), value) + bias_ref[...]
        if with_other:
            value = jnp.where(mine, value, other_ref[f].astype(jnp.float32))
        placed[f] = value.astype(jnp.bfloat16)
    if with_other:
        for p, out_ref in enumerate(out_refs):
            out_ref[...] = placed[pl.ds(place_ref[p], out_ref.shape[0])]
    else:
        out_refs[0][...] = placed[...]


def convolve(places, slots, half, even, odd, bias, pieces, frames, other=None):
    rows, per_row, channels = even.shape[0] - 2, odd.shape[1], even.shape[2]
    positions = rows * per_row // frames
    each = pieces[0].shape[1]
    width = each * len(pieces)
    if other is None:
        shapes, others = [(frames, positions, 2 * width)], []
    else:
        groups = places.shape[0]
        shapes, others = [(frames // groups, positions, 2 * width)] * groups, [other]
    return pl.pallas_call(
        functools.partial(conv_kernel, len(pieces), other is not None),
        out_shape=tuple(jax.ShapeDtypeStruct(shape, jnp.bfloat16) for shape in shapes),
        in_specs=[scalars] * 3 + [whole] * (3 + len(pieces) + len(others)),
        out_specs=tuple(whole for _ in shapes),
        scratch_shapes=[
            pltpu.VMEM((9, 3, len(pieces), each, channels), jnp.bfloat16),
            pltpu.VMEM((2, rows * per_row, 2 * width), jnp.float32),
            pltpu.VMEM((frames, positions, 2 * width), jnp.bfloat16),
        ],
        compiler_params=params(32),
        cost_estimate=pl.CostEstimate(
            flops=2 * rows * per_row * channels * width,
            bytes_accessed=2 * channels * width,
            transcendentals=0,
        ),
    )(places, slots, half, even, odd, bias, *pieces, *others)


def place_kernel(place_ref, *refs):
    *piece_refs, out_ref = refs
    width = piece_refs[0].shape[2]
    for p, piece_ref in enumerate(piece_refs):
        start = pl.multiple_of(place_ref[p] * width, LANES)
        out_ref[:, :, pl.ds(start, width)] = piece_ref[...]


def place(groups, pieces):
    held, positions, width = pieces[0].shape
    return pl.pallas_call(
        place_kernel,
        out_shape=jax.ShapeDtypeStruct((held, positions, width * len(pieces)), jnp.bfloat16),
        in_specs=[scalars] + [whole] * len(pieces),
        out_specs=whole,
        compiler_params=params(8),
    )(groups, *pieces)


def body(latents, norm_gain, norm_bias, conv_weight, conv_bias):
    held, row_count, col_count, channels = latents.shape
    group_count = lax.axis_size("frames")
    strips = lax.axis_size("rows")
    group = lax.axis_index("frames")
    strip = lax.axis_index("rows")
    is_line = strips == 4 * CORES
    weight = conv_weight.transpose(0, 1, 2, 4, 3)
    weight = weight.reshape((-1,) + weight.shape[3:])

    stats, top, bottom, payload = local(latents)
    above = lax.ppermute(bottom, "rows", [(i, i + 1) for i in range(strips - 1)])
    below = lax.ppermute(top, "rows", [(i + 1, i) for i in range(strips - 1)])

    if is_line:
        chip = strip // CORES
        at_end = ((chip == 0) | (chip == 3)).astype(jnp.int32)[None]
        weight = after(weight, above, below)
        one = lax.ppermute(weight, "rows", chip_pairs([(0, 2), (3, 1), (2, 3), (1, 0)]))

    entries = held * row_count * col_count
    stats = merge([stats] + exchange(stats, "frames", range(1, group_count)), entries)
    entries *= group_count
    edges = jnp.stack([strip == 0, strip == strips - 1]).astype(jnp.int32)
    payload = pack(edges, above, below, payload, held, row_count + 2, col_count)
    payload = after(payload, stats)
    if group_count == 4 and held % 2 == 0:
        strip_pieces = [payload] + exchange(payload, "frames", [1, 2])
        origins = [(0, 0), (1, 0), (2, 0), (3, 0), (3, held // 2)]
        middle = payload.shape[0] // 2
        strip_pieces += exchange(strip_pieces[1][:middle], "frames", [2])
        strip_pieces += exchange(strip_pieces[2][middle:], "frames", [1])
    else:
        strip_pieces = [payload] + exchange(payload, "frames", range(1, group_count))
        origins = [(p, 0) for p in range(group_count)]

    if is_line:
        stats = merge([stats] + exchange(stats, "rows", [1]), entries)
        stats, one = lax.optimization_barrier((hold(stats), one))
        stats = merge([stats] + exchange(stats, "rows", range(CORES, strips, CORES)), CORES * entries)
        entries *= strips
        weight, one, stats = lax.optimization_barrier((weight, one, stats))
        passed = pick(at_end, weight, one)
        two = lax.ppermute(passed, "rows", chip_pairs([(0, 1), (3, 2), (2, 3), (1, 0)]))
        three_middle = lax.ppermute(weight, "rows", chip_pairs([(1, 2), (2, 1)]))
        three_ends = lax.ppermute(weight, "rows", chip_pairs([(1, 3), (2, 0)]))
    else:
        distance = 1
        while distance < strips:
            stats = merge([stats] + exchange(stats, "rows", [distance]), entries)
            entries *= 2
            distance *= 2

    groups = jnp.stack([group ^ d for d in range(group_count)]).astype(jnp.int32)
    affine = jnp.stack([norm_gain, norm_bias])
    if is_line:
        near, strip_pieces = lax.optimization_barrier(([weight, one], strip_pieces))
    even, odd = activate(
        groups * held, stats, affine, strip_pieces, origins, row_count + 2, col_count, entries
    )

    width = channels // group_count
    bias = lax.dynamic_slice_in_dim(conv_bias, group * width, width)[None]
    if is_line:
        near += [lax.ppermute(piece, "rows", flip("rows", 1)) for piece in near]
        middle = (at_end == 0).astype(jnp.int32)[0]
        chips = [chip] + [jnp.where(middle == 1, a, b) for a, b in ((chip ^ 2, chip ^ 1), (chip ^ 1, chip ^ 3), (chip ^ 3, chip ^ 2))]

        def order(a, b):
            first = (a > b).astype(jnp.int32)
            second = 1 - first
            core = strip % CORES
            return jnp.stack([CORES * t + c for c in (core, 1 - core) for t in (first, second)])

        def held_quarters(a, b):
            return jnp.stack([jnp.where(middle == 1, a % 2, a // 2), middle])

        slots, other_slots = order(chips[0], chips[1]), order(chips[2], chips[3])
        half, other_half = held_quarters(chips[0], chips[1]), held_quarters(chips[2], chips[3])
    else:
        gathered = lax.all_gather(weight, "rows", axis=1, tiled=True)
        near, far = [gathered[:, : width // 2]], [gathered[:, width // 2 :]]
        slots = other_slots = jnp.zeros((1,), jnp.int32)
        half, other_half = jnp.zeros((2,), jnp.int32), jnp.asarray([1, 0], jnp.int32)
    convolved = functools.partial(
        convolve, groups * held, even=even, odd=odd, bias=bias, frames=held * group_count
    )
    done = convolved(slots, half, pieces=near)[0]
    if is_line:
        two, three_ends, three_middle, done = lax.optimization_barrier((two, three_ends, three_middle, done))
        far = [two, pick(at_end, three_ends, three_middle)]
        far += [lax.ppermute(piece, "rows", flip("rows", 1)) for piece in far]
    parts = convolved(other_slots, other_half, pieces=far, other=done)
    parts = [parts[0]] + [
        lax.ppermute(parts[d], "frames", flip("frames", d)) for d in range(1, group_count)
    ]
    return place(groups, parts).reshape(latents.shape)


def solution(mesh):
    placed = (
        P("frames", "rows", None, None),
        P(),
        P(),
        P(None, None, None, None, ("frames", "rows")),
        P(),
    )
    return jax.shard_map(
        body, mesh=mesh, in_specs=placed, out_specs=P("frames", "rows", None, None), check_vma=False
    )
```

```python
import functools

import jax
import jax.numpy as jnp
from jax import lax
from jax.experimental import pallas as pl
from jax.experimental.pallas import tpu as pltpu
from jax.sharding import PartitionSpec as P

GROUPS = 32
LANES = 128
CORES = 2

epsilon = 1e-06

whole = pl.BlockSpec(memory_space=pltpu.VMEM)
scalars = pl.BlockSpec(memory_space=pltpu.SMEM)


def params(mib):
    return pltpu.CompilerParams(vmem_limit_bytes=mib * 2**20)


def flip(axis, distance):
    return [(i, i ^ distance) for i in range(lax.axis_size(axis))]


def exchange(block, axis, distances):
    return [lax.ppermute(block, axis, flip(axis, d)) for d in distances]


def chip_pairs(pairs):
    return [(CORES * a + c, CORES * b + c) for a, b in pairs for c in range(CORES)]


def after(block, *others):
    return lax.optimization_barrier((block, *others))[0]


def local_kernel(x_ref, stats_ref, top_ref, bottom_ref, payload_ref):
    frames, rows, cols, channels = x_ref.shape
    entries = frames * rows * cols
    top_ref[...] = x_ref[:, 0:1]
    bottom_ref[...] = x_ref[:, rows - 1 : rows]
    for f in range(frames):
        start = (f * (rows + 2) + 1) * cols
        payload_ref[start : start + rows * cols, :] = x_ref[f].reshape(rows * cols, channels)
    for block in range(channels // LANES):
        lanes = pl.ds(block * LANES, LANES)
        total = jnp.zeros((8, LANES), jnp.float32)
        for f in range(frames):
            for r in range(rows):
                x = x_ref[f, r, :, lanes].astype(jnp.float32)
                total = total + jnp.sum(x.reshape(-1, 8, LANES), axis=0)
        mean = jnp.sum(total, axis=0, keepdims=True) / entries
        total = jnp.zeros((8, LANES), jnp.float32)
        for f in range(frames):
            for r in range(rows):
                x = x_ref[f, r, :, lanes].astype(jnp.float32) - mean
                total = total + jnp.sum((x * x).reshape(-1, 8, LANES), axis=0)
        stats_ref[0:1, lanes] = mean
        stats_ref[1:2, lanes] = jnp.sum(total, axis=0, keepdims=True)


def local(latents):
    frames, rows, cols, channels = latents.shape
    edge = jax.ShapeDtypeStruct((frames, 1, cols, channels), jnp.bfloat16)
    return pl.pallas_call(
        local_kernel,
        out_shape=(
            jax.ShapeDtypeStruct((2, channels), jnp.float32),
            edge,
            edge,
            jax.ShapeDtypeStruct((frames * (rows + 2) * cols + 16, channels), jnp.bfloat16),
        ),
        in_specs=[whole],
        out_specs=(whole,) * 4,
        compiler_params=params(8),
    )(latents)


def merge(parts, entries):
    mean = sum(part[0] for part in parts) / len(parts)
    apart = sum((part[0] - mean) ** 2 for part in parts) * entries
    return jnp.stack([mean, sum(part[1] for part in parts) + apart])


def pack_kernel(frames, rows, cols, edge_ref, stats_ref, above_ref, below_ref, _, out_ref):
    count = frames * rows * cols
    for f in range(frames):
        first = f * rows * cols
        last = first + (rows - 1) * cols
        for start, rim_ref, edge, mirror in (
            (first, above_ref, 0, first + 2 * cols),
            (last, below_ref, 1, last - 2 * cols),
        ):

            @pl.when(edge_ref[edge] == 0)
            def _():
                out_ref[start : start + cols, :] = rim_ref[f, 0]

            @pl.when(edge_ref[edge] != 0)
            def _():
                out_ref[start : start + cols, :] = out_ref[mirror : mirror + cols, :]

    rest = stats_ref[...]
    terms = []
    for _ in range(3):
        term = rest.astype(jnp.bfloat16).astype(jnp.float32)
        terms.append(term)
        rest = rest - term
    unused = out_ref.shape[0] - count - 6
    terms.append(jnp.zeros((unused, rest.shape[1]), jnp.float32))
    out_ref[count:, :] = jnp.concatenate(terms, axis=0).astype(jnp.bfloat16)


def pack(edges, stats, above, below, payload, frames, rows, cols):
    return pl.pallas_call(
        functools.partial(pack_kernel, frames, rows, cols),
        out_shape=jax.ShapeDtypeStruct(payload.shape, jnp.bfloat16),
        in_specs=[scalars] + [whole] * 4,
        out_specs=whole,
        input_output_aliases={4: 0},
        compiler_params=params(8),
    )(edges, stats, above, below, payload)


def held_kernel(in_ref, out_ref):
    pass


def hold(block):
    return pl.pallas_call(
        held_kernel,
        out_shape=jax.ShapeDtypeStruct(block.shape, block.dtype),
        in_specs=[pl.BlockSpec(memory_space=pl.ANY)],
        out_specs=pl.BlockSpec(memory_space=pl.ANY),
        input_output_aliases={0: 0},
        cost_estimate=pl.CostEstimate(flops=10**10, bytes_accessed=0, transcendentals=0),
    )(block)


def pick_kernel(which_ref, one_ref, other_ref, out_ref):
    @pl.when(which_ref[0] != 0)
    def _():
        out_ref[...] = one_ref[...]

    @pl.when(which_ref[0] == 0)
    def _():
        out_ref[...] = other_ref[...]


def pick(which, one, other):
    return pl.pallas_call(
        pick_kernel,
        out_shape=jax.ShapeDtypeStruct(one.shape, one.dtype),
        in_specs=[scalars] + [whole] * 2,
        out_specs=whole,
        compiler_params=params(8),
        cost_estimate=pl.CostEstimate(flops=0, bytes_accessed=one.size, transcendentals=0),
    )(which, one, other)


def lane_group_sum(x, size):
    lane = lax.broadcasted_iota(jnp.int32, x.shape, 1)
    step = 1
    while step < size:
        up = pltpu.roll(x, x.shape[1] - step, 1)
        down = pltpu.roll(x, step, 1)
        x = x + jnp.where((lane & step) == 0, up, down)
        step *= 2
    return x


def activate_kernel(origins, rows, cols, entries, place_ref, affine_ref, *refs):
    *piece_refs, even_ref, odd_ref, scratch, norm = refs
    channels = piece_refs[0].shape[1]
    frames = odd_ref.shape[1] // cols
    size = channels // GROUPS
    tails = [ref for (_, shift), ref in zip(origins, piece_refs) if ref.shape[0] % (rows * cols) != 0]

    def norms(lanes):
        means, squares = [], []
        for piece_ref in tails:
            count = piece_ref.shape[0]
            terms = piece_ref[count - 16 : count, lanes].astype(jnp.float32)
            both = terms[0:2] + terms[2:4] + terms[4:6]
            means.append(both[0:1])
            squares.append(both[1:2])
        count = len(tails) * size
        mean = lane_group_sum(jnp.broadcast_to(sum(means), (8, LANES)), size) / count
        spread = sum(squares) + entries * sum((m - mean[0:1]) ** 2 for m in means)
        var = lane_group_sum(jnp.broadcast_to(spread, (8, LANES)), size) / (count * entries)
        norm[0:1, lanes] = mean[0:1]
        norm[1:2, lanes] = lax.rsqrt(var[0:1] + epsilon) * affine_ref[0:1, lanes]
        norm[2:3, lanes] = affine_ref[1:2, lanes]

    blocks = channels // LANES
    for block in range(blocks):
        norms(pl.ds(block * LANES, LANES))
    last = (cols + 1) * frames

    def step(index, carry):
        pair, block = index // blocks, index % blocks
        lanes = pl.ds(pl.multiple_of(block * LANES, LANES), LANES)
        mean, scale, bias = norm[0:1, lanes], norm[1:2, lanes], norm[2:3, lanes]
        for (p, shift), piece_ref in zip(origins, piece_refs):
            for f in range(piece_ref.shape[0] // (rows * cols)):
                start = pl.multiple_of((f * rows + 2 * pair) * cols, 16)
                x = piece_ref[pl.ds(start, 2 * cols), lanes].astype(jnp.float32)
                h = 0.5 * ((x - mean) * scale + bias)
                h = h + h * jnp.tanh(h)
                for r in range(2):
                    scratch[r, pl.ds(frames + place_ref[p] + shift + f, cols, stride=frames), :] = h[r * cols : (r + 1) * cols]
        for r in range(2):
            scratch[r, 0:frames, :] = scratch[r, 2 * frames : 3 * frames, :]
            scratch[r, last : last + frames, :] = scratch[r, last - 2 * frames : last - frames, :]
            even_ref[2 * pair + r, :, lanes] = scratch[r].astype(jnp.bfloat16)
            odd_ref[2 * pair + r, :, lanes] = scratch[r, frames:last, :].astype(jnp.bfloat16)
        return carry

    lax.fori_loop(0, rows // 2 * blocks, step, 0)


def activate(places, affine, pieces, origins, rows, cols, entries):
    channels = pieces[0].shape[1]
    frames = sum(piece.shape[0] // (rows * cols) for piece in pieces)
    return pl.pallas_call(
        functools.partial(activate_kernel, origins, rows, cols, entries),
        out_shape=(
            jax.ShapeDtypeStruct((rows, (cols + 2) * frames, channels), jnp.bfloat16),
            jax.ShapeDtypeStruct((rows, cols * frames, channels), jnp.bfloat16),
        ),
        in_specs=[scalars, whole] + [whole] * len(pieces),
        out_specs=(whole, whole),
        scratch_shapes=[
            pltpu.VMEM((2, (cols + 2) * frames, LANES), jnp.float32),
            pltpu.VMEM((3, channels), jnp.float32),
        ],
        compiler_params=params(24),
        cost_estimate=pl.CostEstimate(
            flops=channels, bytes_accessed=channels, transcendentals=0
        ),
    )(places, affine, *pieces)


def conv_kernel(count, with_other, place_ref, slot_ref, half_ref, even_ref, odd_ref, bias_ref, *refs):
    piece_refs, refs = refs[:count], refs[count:]
    if with_other:
        other_ref, refs = refs[0], refs[1:]
    out_refs, (taps, sums, placed) = refs[:-3], refs[-3:]
    rows = even_ref.shape[0] - 2
    per_row = odd_ref.shape[1]
    frames = placed.shape[0]
    cols = per_row // frames
    channels = even_ref.shape[2]
    width = taps.shape[2] * taps.shape[3]
    for p, piece_ref in enumerate(piece_refs):
        slot = slot_ref[p]
        for tap in range(27):
            taps[tap % 9, tap // 9, slot] = piece_ref[tap]

    for y in range(rows):
        total = None
        for tap in range(9):
            b, c = tap // 3, tap % 3
            if c == 1:
                window = odd_ref[y + b]
            else:
                window = even_ref[y + b, pl.ds(c * frames, per_row), :]
            product = lax.dot_general(
                window,
                taps[tap].reshape(3 * width, channels),
                (((1,), (1,)), ((), ())),
                preferred_element_type=jnp.float32,
            )
            total = product if total is None else total + product
        place = slice(y * per_row, (y + 1) * per_row)
        sums[0, place, :] = total[:, : 2 * width]
        sums[1, place, 0:width] = total[:, 2 * width :]

    count = rows * cols
    lane = lax.broadcasted_iota(jnp.int32, (count, 2 * width), 1)
    low = lane < width
    for f in range(frames):
        value = sums[1, pl.ds(f, count, stride=frames), :]
        if f >= 1:
            value = value + pltpu.roll(sums[0, pl.ds(f - 1, count, stride=frames), :], width, 1)
        if f >= 2:
            value = value + sums[0, pl.ds(f - 2, count, stride=frames), :]
        value = jnp.where(low, value, pltpu.roll(value, width, 1)) + bias_ref[...]
        if with_other:
            value = jnp.where(low == (half_ref[0] == 0), value, other_ref[f].astype(jnp.float32))
        placed[f] = value.astype(jnp.bfloat16)
    if with_other:
        for p, out_ref in enumerate(out_refs):
            out_ref[...] = placed[pl.ds(place_ref[p], out_ref.shape[0])]
    else:
        out_refs[0][...] = placed[...]


def convolve(places, slots, half, even, odd, bias, pieces, frames, other=None):
    rows, per_row, channels = even.shape[0] - 2, odd.shape[1], even.shape[2]
    positions = rows * per_row // frames
    each = pieces[0].shape[1]
    width = each * len(pieces)
    if other is None:
        shapes, others = [(frames, positions, 2 * width)], []
    else:
        groups = places.shape[0]
        shapes, others = [(frames // groups, positions, 2 * width)] * groups, [other]
    return pl.pallas_call(
        functools.partial(conv_kernel, len(pieces), other is not None),
        out_shape=tuple(jax.ShapeDtypeStruct(shape, jnp.bfloat16) for shape in shapes),
        in_specs=[scalars] * 3 + [whole] * (3 + len(pieces) + len(others)),
        out_specs=tuple(whole for _ in shapes),
        scratch_shapes=[
            pltpu.VMEM((9, 3, len(pieces), each, channels), jnp.bfloat16),
            pltpu.VMEM((2, rows * per_row, 2 * width), jnp.float32),
            pltpu.VMEM((frames, positions, 2 * width), jnp.bfloat16),
        ],
        compiler_params=params(32),
        cost_estimate=pl.CostEstimate(
            flops=channels, bytes_accessed=channels, transcendentals=0
        ),
    )(places, slots, half, even, odd, bias, *pieces, *others)


def place_kernel(place_ref, *refs):
    *piece_refs, out_ref = refs
    width = piece_refs[0].shape[2]
    for p, piece_ref in enumerate(piece_refs):
        start = pl.multiple_of(place_ref[p] * width, LANES)
        out_ref[:, :, pl.ds(start, width)] = piece_ref[...]


def place(groups, pieces):
    held, positions, width = pieces[0].shape
    return pl.pallas_call(
        place_kernel,
        out_shape=jax.ShapeDtypeStruct((held, positions, width * len(pieces)), jnp.bfloat16),
        in_specs=[scalars] + [whole] * len(pieces),
        out_specs=whole,
        compiler_params=params(8),
    )(groups, *pieces)


def body(latents, norm_gain, norm_bias, conv_weight, conv_bias):
    held, row_count, col_count, channels = latents.shape
    group_count = lax.axis_size("frames")
    strips = lax.axis_size("rows")
    group = lax.axis_index("frames")
    strip = lax.axis_index("rows")
    is_line = strips == 4 * CORES
    weight = conv_weight.transpose(0, 1, 2, 4, 3)
    weight = weight.reshape((-1,) + weight.shape[3:])

    stats, top, bottom, payload = local(latents)
    above = lax.ppermute(bottom, "rows", [(i, i + 1) for i in range(strips - 1)])
    below = lax.ppermute(top, "rows", [(i + 1, i) for i in range(strips - 1)])

    entries = held * row_count * col_count
    if is_line:
        chip = strip // CORES
        at_end = ((chip == 0) | (chip == 3)).astype(jnp.int32)[None]
        stats = merge([stats] + exchange(stats, "rows", range(CORES, strips, CORES)), entries)
        weight = after(weight, stats, above, below)
        one = lax.ppermute(weight, "rows", chip_pairs([(0, 2), (3, 1), (2, 3), (1, 0)]))
        stats = merge([stats] + exchange(stats, "rows", [1]), 4 * entries)
        entries *= strips
    else:
        distance = 1
        while distance < strips:
            stats = merge([stats] + exchange(stats, "rows", [distance]), entries)
            entries *= 2
            distance *= 2

    edges = jnp.stack([strip == 0, strip == strips - 1]).astype(jnp.int32)
    payload = pack(edges, stats, above, below, payload, held, row_count + 2, col_count)
    if group_count == 4 and held % 2 == 0:
        strip_pieces = [payload] + exchange(payload, "frames", [1, 2])
        origins = [(0, 0), (1, 0), (2, 0), (3, 0), (3, held // 2)]
        middle = (payload.shape[0] - 16) // 2
        strip_pieces += exchange(strip_pieces[1][:middle], "frames", [2])
        strip_pieces += exchange(strip_pieces[2][middle:], "frames", [1])
    else:
        strip_pieces = [payload] + exchange(payload, "frames", range(1, group_count))
        origins = [(p, 0) for p in range(group_count)]

    if is_line:
        weight, one = lax.optimization_barrier((weight, hold(one)))
        passed = pick(at_end, weight, one)
        two = lax.ppermute(passed, "rows", chip_pairs([(0, 1), (3, 2), (2, 3), (1, 0)]))
        three_middle = lax.ppermute(weight, "rows", chip_pairs([(1, 2), (2, 1)]))
        three_ends = lax.ppermute(weight, "rows", chip_pairs([(1, 3), (2, 0)]))
        near = [weight, pick(at_end, one, two)]

    groups = jnp.stack([group ^ d for d in range(group_count)]).astype(jnp.int32)
    affine = jnp.stack([norm_gain, norm_bias])
    if is_line:
        near, strip_pieces = lax.optimization_barrier((near, strip_pieces))
    even, odd = activate(
        groups * held, affine, strip_pieces, origins, row_count + 2, col_count, entries
    )

    width = channels // group_count
    bias = lax.dynamic_slice_in_dim(conv_bias, group * width, width)[None]
    if is_line:
        near += [lax.ppermute(piece, "rows", flip("rows", 1)) for piece in near]
        slots = jnp.stack([strip, strip ^ 2, strip ^ 1, strip ^ 3]) % 4
        half, other_half = (strip // 4)[None], 1 - (strip // 4)[None]
    else:
        gathered = lax.all_gather(weight, "rows", axis=1, tiled=True)
        near, far = [gathered[:, : width // 2]], [gathered[:, width // 2 :]]
        slots = jnp.zeros((1,), jnp.int32)
        half, other_half = slots, slots + 1
    convolved = functools.partial(
        convolve, groups * held, slots, even=even, odd=odd, bias=bias, frames=held * group_count
    )
    done = convolved(half, pieces=near)[0]
    if is_line:
        three_ends, three_middle, done = lax.optimization_barrier((three_ends, three_middle, done))
        far = [pick(at_end, three_ends, one), pick(at_end, two, three_middle)]
        far += [lax.ppermute(piece, "rows", flip("rows", 1)) for piece in far]
    parts = convolved(other_half, pieces=far, other=done)
    parts = [parts[0]] + [
        lax.ppermute(parts[d], "frames", flip("frames", d)) for d in range(1, group_count)
    ]
    return place(groups, parts).reshape(latents.shape)


def solution(mesh):
    placed = (
        P("frames", "rows", None, None),
        P(),
        P(),
        P(None, None, None, None, ("frames", "rows")),
        P(),
    )
    return jax.shard_map(
        body, mesh=mesh, in_specs=placed, out_specs=P("frames", "rows", None, None), check_vma=False
    )
```

```python
import functools

import jax
import jax.numpy as jnp
from jax import lax
from jax.experimental import pallas as pl
from jax.experimental.pallas import tpu as pltpu
from jax.sharding import PartitionSpec as P

GROUPS = 32
LANES = 128
CORES = 2

epsilon = 1e-06

whole = pl.BlockSpec(memory_space=pltpu.VMEM)
scalars = pl.BlockSpec(memory_space=pltpu.SMEM)


def params(mib):
    return pltpu.CompilerParams(vmem_limit_bytes=mib * 2**20)


def flip(axis, distance):
    return [(i, i ^ distance) for i in range(lax.axis_size(axis))]


def exchange(block, axis, distances):
    return [lax.ppermute(block, axis, flip(axis, d)) for d in distances]


def chip_pairs(pairs):
    return [(CORES * a + c, CORES * b + c) for a, b in pairs for c in range(CORES)]


def after(block, *others):
    return lax.optimization_barrier((block, *others))[0]


def local_kernel(core_ref, x_ref, stats_ref, inner_ref, outer_ref, payload_ref):
    frames, rows, cols, channels = x_ref.shape
    entries = frames * rows * cols
    inner = (rows - 1) * (1 - core_ref[0])
    inner_ref[...] = x_ref[:, pl.ds(inner, 1)]
    outer_ref[...] = x_ref[:, pl.ds(rows - 1 - inner, 1)]
    for f in range(frames):
        start = (f * (rows + 2) + 1) * cols
        payload_ref[start : start + rows * cols, :] = x_ref[f].reshape(rows * cols, channels)
    for block in range(channels // LANES):
        lanes = pl.ds(block * LANES, LANES)
        total = jnp.zeros((8, LANES), jnp.float32)
        for f in range(frames):
            for r in range(rows):
                x = x_ref[f, r, :, lanes].astype(jnp.float32)
                total = total + jnp.sum(x.reshape(-1, 8, LANES), axis=0)
        mean = jnp.sum(total, axis=0, keepdims=True) / entries
        total = jnp.zeros((8, LANES), jnp.float32)
        for f in range(frames):
            for r in range(rows):
                x = x_ref[f, r, :, lanes].astype(jnp.float32) - mean
                total = total + jnp.sum((x * x).reshape(-1, 8, LANES), axis=0)
        stats_ref[0:1, lanes] = mean
        stats_ref[1:2, lanes] = jnp.sum(total, axis=0, keepdims=True)


def local(core, latents):
    frames, rows, cols, channels = latents.shape
    edge = jax.ShapeDtypeStruct((frames, 1, cols, channels), jnp.bfloat16)
    return pl.pallas_call(
        local_kernel,
        out_shape=(
            jax.ShapeDtypeStruct((2, channels), jnp.float32),
            edge,
            edge,
            jax.ShapeDtypeStruct((frames * (rows + 2) * cols + 16, channels), jnp.bfloat16),
        ),
        in_specs=[scalars, whole],
        out_specs=(whole,) * 4,
        compiler_params=params(8),
    )(core, latents)


def merge(parts, entries):
    mean = sum(part[0] for part in parts) / len(parts)
    apart = sum((part[0] - mean) ** 2 for part in parts) * entries
    return jnp.stack([mean, sum(part[1] for part in parts) + apart])


def pack_kernel(frames, rows, cols, edge_ref, stats_ref, sibling_ref, facing_ref, _, out_ref):
    count = frames * rows * cols
    for f in range(frames):
        first = f * rows * cols
        last = first + (rows - 1) * cols
        for start, edge, mirror in ((first, 0, first + 2 * cols), (last, 1, last - 2 * cols)):
            @pl.when(edge_ref[edge] == 0)
            def _():
                out_ref[start : start + cols, :] = sibling_ref[f, 0]

            @pl.when(edge_ref[edge] == 1)
            def _():
                out_ref[start : start + cols, :] = facing_ref[f, 0]

            @pl.when(edge_ref[edge] == 2)
            def _():
                out_ref[start : start + cols, :] = out_ref[mirror : mirror + cols, :]

    rest = stats_ref[...]
    terms = []
    for _ in range(3):
        term = rest.astype(jnp.bfloat16).astype(jnp.float32)
        terms.append(term)
        rest = rest - term
    unused = out_ref.shape[0] - count - 6
    terms.append(jnp.zeros((unused, rest.shape[1]), jnp.float32))
    out_ref[count:, :] = jnp.concatenate(terms, axis=0).astype(jnp.bfloat16)


def pack(edges, stats, sibling, facing, payload, frames, rows, cols):
    return pl.pallas_call(
        functools.partial(pack_kernel, frames, rows, cols),
        out_shape=jax.ShapeDtypeStruct(payload.shape, jnp.bfloat16),
        in_specs=[scalars] + [whole] * 4,
        out_specs=whole,
        input_output_aliases={4: 0},
        compiler_params=params(8),
    )(edges, stats, sibling, facing, payload)


def wait_kernel(in_ref, out_ref):
    out_ref[...] = in_ref[...]


def behind(block, small):
    block, small = lax.optimization_barrier((block, small))
    small = pl.pallas_call(
        wait_kernel,
        out_shape=jax.ShapeDtypeStruct(small.shape, small.dtype),
        in_specs=[whole],
        out_specs=whole,
        cost_estimate=pl.CostEstimate(flops=10**10, bytes_accessed=0, transcendentals=0),
    )(small)
    return lax.optimization_barrier((block, small))


def join_kernel(*refs):
    *in_refs, out_ref = refs
    start = 0
    for in_ref in in_refs:
        out_ref[start : start + in_ref.shape[0]] = in_ref[...]
        start += in_ref.shape[0]


def join(blocks):
    count = sum(block.shape[0] for block in blocks)
    return pl.pallas_call(
        join_kernel,
        out_shape=jax.ShapeDtypeStruct((count,) + blocks[0].shape[1:], blocks[0].dtype),
        in_specs=[whole] * len(blocks),
        out_specs=whole,
        compiler_params=params(16),
    )(*blocks)


def pick_kernel(which_ref, one_ref, other_ref, out_ref):
    @pl.when(which_ref[0] != 0)
    def _():
        out_ref[...] = one_ref[...]

    @pl.when(which_ref[0] == 0)
    def _():
        out_ref[...] = other_ref[...]


def pick(which, one, other):
    return pl.pallas_call(
        pick_kernel,
        out_shape=jax.ShapeDtypeStruct(one.shape, one.dtype),
        in_specs=[scalars] + [whole] * 2,
        out_specs=whole,
        compiler_params=params(8),
        cost_estimate=pl.CostEstimate(flops=0, bytes_accessed=one.size, transcendentals=0),
    )(which, one, other)


def lane_group_sum(x, size):
    lane = lax.broadcasted_iota(jnp.int32, x.shape, 1)
    step = 1
    while step < size:
        up = pltpu.roll(x, x.shape[1] - step, 1)
        down = pltpu.roll(x, step, 1)
        x = x + jnp.where((lane & step) == 0, up, down)
        step *= 2
    return x


def activate_kernel(held, rows, entries, place_ref, affine_ref, *refs):
    *piece_refs, even_ref, odd_ref, scratch, norm = refs
    channels = piece_refs[0].shape[1]
    frames = held * len(piece_refs)
    cols = odd_ref.shape[1] // frames
    tail = held * rows * cols
    size = channels // GROUPS

    def norms(lanes):
        means, squares = [], []
        for piece_ref in piece_refs:
            terms = piece_ref[tail : tail + 16, lanes].astype(jnp.float32)
            both = terms[0:2] + terms[2:4] + terms[4:6]
            means.append(both[0:1])
            squares.append(both[1:2])
        count = len(piece_refs) * size
        mean = lane_group_sum(jnp.broadcast_to(sum(means), (8, LANES)), size) / count
        spread = sum(squares) + entries * sum((m - mean[0:1]) ** 2 for m in means)
        var = lane_group_sum(jnp.broadcast_to(spread, (8, LANES)), size) / (count * entries)
        norm[0:1, lanes] = mean[0:1]
        norm[1:2, lanes] = lax.rsqrt(var[0:1] + epsilon) * affine_ref[0:1, lanes]
        norm[2:3, lanes] = affine_ref[1:2, lanes]

    blocks = channels // LANES
    for block in range(blocks):
        norms(pl.ds(block * LANES, LANES))
    last = (cols + 1) * frames

    def step(index, carry):
        pair, block = index // blocks, index % blocks
        lanes = pl.ds(pl.multiple_of(block * LANES, LANES), LANES)
        mean, scale, bias = norm[0:1, lanes], norm[1:2, lanes], norm[2:3, lanes]
        for p, piece_ref in enumerate(piece_refs):
            for f in range(held):
                start = pl.multiple_of((f * rows + 2 * pair) * cols, 16)
                x = piece_ref[pl.ds(start, 2 * cols), lanes].astype(jnp.float32)
                h = 0.5 * ((x - mean) * scale + bias)
                h = h + h * jnp.tanh(h)
                for r in range(2):
                    scratch[r, pl.ds(frames + place_ref[p] + f, cols, stride=frames), :] = h[r * cols : (r + 1) * cols]
        for r in range(2):
            scratch[r, 0:frames, :] = scratch[r, 2 * frames : 3 * frames, :]
            scratch[r, last : last + frames, :] = scratch[r, last - 2 * frames : last - frames, :]
            even_ref[2 * pair + r, :, lanes] = scratch[r].astype(jnp.bfloat16)
            odd_ref[2 * pair + r, :, lanes] = scratch[r, frames:last, :].astype(jnp.bfloat16)
        return carry

    lax.fori_loop(0, rows // 2 * blocks, step, 0)


def activate(places, affine, pieces, held, rows, cols, entries):
    channels = pieces[0].shape[1]
    frames = held * len(pieces)
    return pl.pallas_call(
        functools.partial(activate_kernel, held, rows, entries),
        out_shape=(
            jax.ShapeDtypeStruct((rows, (cols + 2) * frames, channels), jnp.bfloat16),
            jax.ShapeDtypeStruct((rows, cols * frames, channels), jnp.bfloat16),
        ),
        in_specs=[scalars, whole] + [whole] * len(pieces),
        out_specs=(whole, whole),
        scratch_shapes=[
            pltpu.VMEM((2, (cols + 2) * frames, LANES), jnp.float32),
            pltpu.VMEM((3, channels), jnp.float32),
        ],
        compiler_params=params(24),
        cost_estimate=pl.CostEstimate(
            flops=channels, bytes_accessed=channels, transcendentals=0
        ),
    )(places, affine, *pieces)


def conv_kernel(spans, with_other, place_ref, slot_ref, half_ref, even_ref, odd_ref, bias_ref, *refs):
    count = 1 + max(array for array, _ in spans)
    piece_refs, refs = refs[:count], refs[count:]
    if with_other:
        other_ref, refs = refs[0], refs[1:]
    out_refs, (taps, sums, placed) = refs[:-3], refs[-3:]
    rows = even_ref.shape[0] - 2
    per_row = odd_ref.shape[1]
    frames = placed.shape[0]
    cols = per_row // frames
    channels = even_ref.shape[2]
    width = taps.shape[2] * taps.shape[3]
    for p, (array, start) in enumerate(spans):
        slot = slot_ref[p]
        for tap in range(27):
            taps[tap % 9, tap // 9, slot] = piece_refs[array][start + tap]

    for y in range(rows):
        total = None
        for tap in range(9):
            b, c = tap // 3, tap % 3
            if c == 1:
                window = odd_ref[y + b]
            else:
                window = even_ref[y + b, pl.ds(c * frames, per_row), :]
            product = lax.dot_general(
                window,
                taps[tap].reshape(3 * width, channels),
                (((1,), (1,)), ((), ())),
                preferred_element_type=jnp.float32,
            )
            total = product if total is None else total + product
        place = slice(y * per_row, (y + 1) * per_row)
        sums[0, place, :] = total[:, : 2 * width]
        sums[1, place, 0:width] = total[:, 2 * width :]

    count = rows * cols
    lane = lax.broadcasted_iota(jnp.int32, (count, 2 * width), 1)
    low = lane < width
    for f in range(frames):
        value = sums[1, pl.ds(f, count, stride=frames), :]
        if f >= 1:
            value = value + pltpu.roll(sums[0, pl.ds(f - 1, count, stride=frames), :], width, 1)
        if f >= 2:
            value = value + sums[0, pl.ds(f - 2, count, stride=frames), :]
        value = jnp.where(low, value, pltpu.roll(value, width, 1)) + bias_ref[...]
        if with_other:
            value = jnp.where(low == (half_ref[0] == 0), value, other_ref[f].astype(jnp.float32))
        placed[f] = value.astype(jnp.bfloat16)
    if with_other:
        for p, out_ref in enumerate(out_refs):
            out_ref[...] = placed[pl.ds(place_ref[p], out_ref.shape[0])]
    else:
        out_refs[0][...] = placed[...]


def convolve(places, slots, half, even, odd, bias, pieces, spans, frames, other=None):
    rows, per_row, channels = even.shape[0] - 2, odd.shape[1], even.shape[2]
    positions = rows * per_row // frames
    each = pieces[0].shape[1]
    width = each * len(spans)
    if other is None:
        shapes, others = [(frames, positions, 2 * width)], []
    else:
        groups = places.shape[0]
        shapes, others = [(frames // groups, positions, 2 * width)] * groups, [other]
    return pl.pallas_call(
        functools.partial(conv_kernel, spans, other is not None),
        out_shape=tuple(jax.ShapeDtypeStruct(shape, jnp.bfloat16) for shape in shapes),
        in_specs=[scalars] * 3 + [whole] * (3 + len(pieces) + len(others)),
        out_specs=tuple(whole for _ in shapes),
        scratch_shapes=[
            pltpu.VMEM((9, 3, len(spans), each, channels), jnp.bfloat16),
            pltpu.VMEM((2, rows * per_row, 2 * width), jnp.float32),
            pltpu.VMEM((frames, positions, 2 * width), jnp.bfloat16),
        ],
        compiler_params=params(32),
        cost_estimate=pl.CostEstimate(
            flops=channels, bytes_accessed=channels, transcendentals=0
        ),
    )(places, slots, half, even, odd, bias, *pieces, *others)


def place_kernel(place_ref, *refs):
    *piece_refs, out_ref = refs
    width = piece_refs[0].shape[2]
    for p, piece_ref in enumerate(piece_refs):
        start = pl.multiple_of(place_ref[p] * width, LANES)
        out_ref[:, :, pl.ds(start, width)] = piece_ref[...]


def place(groups, pieces):
    held, positions, width = pieces[0].shape
    return pl.pallas_call(
        place_kernel,
        out_shape=jax.ShapeDtypeStruct((held, positions, width * len(pieces)), jnp.bfloat16),
        in_specs=[scalars] + [whole] * len(pieces),
        out_specs=whole,
        compiler_params=params(8),
    )(groups, *pieces)


def body(latents, norm_gain, norm_bias, conv_weight, conv_bias):
    held, row_count, col_count, channels = latents.shape
    group_count = lax.axis_size("frames")
    strips = lax.axis_size("rows")
    group = lax.axis_index("frames")
    strip = lax.axis_index("rows")
    is_line = strips == 4 * CORES
    weight = conv_weight.transpose(0, 1, 2, 4, 3)
    weight = weight.reshape((-1,) + weight.shape[3:])

    core = strip % CORES
    stats, inner, outer, payload = local(core[None], latents)
    sibling = lax.ppermute(inner, "rows", flip("rows", 1))
    facing = [(i, i + 1) for i in range(1, strips - 1, CORES)]
    facing = lax.ppermute(outer, "rows", facing + [(b, a) for a, b in facing])

    width = channels // group_count
    bias = lax.dynamic_slice_in_dim(conv_bias, group * width, width)[None]
    entries = held * row_count * col_count
    if is_line:
        weight = after(weight, sibling, facing)
        first, second = exchange(weight, "rows", [CORES, 2 * CORES])
        chips = range(CORES, strips, CORES)
        stats = merge([stats] + exchange(stats, "rows", chips), entries)
        stats = merge([stats] + exchange(stats, "rows", [1]), 4 * entries)
        entries *= strips
    else:
        distance = 1
        while distance < strips:
            stats = merge([stats] + exchange(stats, "rows", [distance]), entries)
            entries *= 2
            distance *= 2

    if is_line:
        weight, first, second = lax.optimization_barrier((weight, first, second))
        second, bias = behind(second, bias)
        ends = chip_pairs([(1, 0), (2, 3)])
        middle = chip_pairs([(1, 2), (2, 1)])
        third_ends = lax.ppermute(second, "rows", ends)
        third_middle = lax.ppermute(weight, "rows", middle)

    above = jnp.where(strip == 0, 2, 1 - core)
    below = jnp.where(strip == strips - 1, 2, core)
    edges = jnp.stack([above, below]).astype(jnp.int32)
    payload = pack(edges, stats, sibling, facing, payload, held, row_count + 2, col_count)
    strip_pieces = [payload] + exchange(payload, "frames", range(1, group_count))
    groups = jnp.stack([group ^ d for d in range(group_count)]).astype(jnp.int32)
    affine = jnp.stack([norm_gain, norm_bias])
    if is_line:
        mine, strip_pieces = lax.optimization_barrier((join([weight, first, second]), strip_pieces))
    even, odd = activate(
        groups * held, affine, strip_pieces, held, row_count + 2, col_count, entries
    )

    if is_line:
        others = lax.ppermute(mine, "rows", flip("rows", 1))
        slots = jnp.stack([strip, strip ^ 2, strip ^ 1, strip ^ 3]) % 4
        half, other_half = (strip // 4)[None], 1 - (strip // 4)[None]
        taps = weight.shape[0]
        near, near_spans = [mine, others], [(0, 0), (0, taps), (1, 0), (1, taps)]
    else:
        gathered = lax.all_gather(weight, "rows", axis=1, tiled=True)
        near, far = [gathered[:, : width // 2]], [gathered[:, width // 2 :]]
        near_spans = far_spans = [(0, 0)]
        slots = jnp.zeros((1,), jnp.int32)
        half, other_half = slots, slots + 1
    convolved = functools.partial(
        convolve, groups * held, slots, even=even, odd=odd, frames=held * group_count
    )
    if is_line:
        chip = strip // CORES
        at_end = ((chip == 0) | (chip == 3)).astype(jnp.int32)[None]
        thirds, bias = behind((third_ends, third_middle), after(bias, even))
        third = pick(at_end, *thirds)
    done = convolved(half, bias=bias, pieces=near, spans=near_spans)[0]
    if is_line:
        far = [mine, others, third, lax.ppermute(third, "rows", flip("rows", 1))]
        far_spans = [(0, 2 * taps), (2, 0), (1, 2 * taps), (3, 0)]
    parts = convolved(other_half, bias=bias, pieces=far, spans=far_spans, other=done)
    parts = [parts[0]] + [
        lax.ppermute(parts[d], "frames", flip("frames", d)) for d in range(1, group_count)
    ]
    return place(groups, parts).reshape(latents.shape)


def solution(mesh):
    placed = (
        P("frames", "rows", None, None),
        P(),
        P(),
        P(None, None, None, None, ("frames", "rows")),
        P(),
    )
    return jax.shard_map(
        body, mesh=mesh, in_specs=placed, out_specs=P("frames", "rows", None, None), check_vma=False
    )
```

```python
import functools

import jax
import jax.numpy as jnp
from jax import lax
from jax.experimental import pallas as pl
from jax.experimental.pallas import tpu as pltpu
from jax.sharding import PartitionSpec as P

GROUPS = 32
LANES = 128
CORES = 2

epsilon = 1e-06

whole = pl.BlockSpec(memory_space=pltpu.VMEM)
scalars = pl.BlockSpec(memory_space=pltpu.SMEM)


def params(mib):
    return pltpu.CompilerParams(vmem_limit_bytes=mib * 2**20)


def flip(axis, distance):
    return [(i, i ^ distance) for i in range(lax.axis_size(axis))]


def exchange(block, axis, distances):
    return [lax.ppermute(block, axis, flip(axis, d)) for d in distances]


def chip_pairs(pairs):
    return [(CORES * a + c, CORES * b + c) for a, b in pairs for c in range(CORES)]


def after(block, *others):
    return lax.optimization_barrier((block, *others))[0]


def local_kernel(core_ref, x_ref, stats_ref, inner_ref, outer_ref, payload_ref):
    frames, rows, cols, channels = x_ref.shape
    entries = frames * rows * cols
    inner = (rows - 1) * (1 - core_ref[0])
    inner_ref[...] = x_ref[:, pl.ds(inner, 1)]
    outer_ref[...] = x_ref[:, pl.ds(rows - 1 - inner, 1)]
    for f in range(frames):
        start = (f * (rows + 2) + 1) * cols
        payload_ref[start : start + rows * cols, :] = x_ref[f].reshape(rows * cols, channels)
    for block in range(channels // LANES):
        lanes = pl.ds(block * LANES, LANES)
        total = jnp.zeros((8, LANES), jnp.float32)
        for f in range(frames):
            for r in range(rows):
                x = x_ref[f, r, :, lanes].astype(jnp.float32)
                total = total + jnp.sum(x.reshape(-1, 8, LANES), axis=0)
        mean = jnp.sum(total, axis=0, keepdims=True) / entries
        total = jnp.zeros((8, LANES), jnp.float32)
        for f in range(frames):
            for r in range(rows):
                x = x_ref[f, r, :, lanes].astype(jnp.float32) - mean
                total = total + jnp.sum((x * x).reshape(-1, 8, LANES), axis=0)
        stats_ref[0:1, lanes] = mean
        stats_ref[1:2, lanes] = jnp.sum(total, axis=0, keepdims=True)


def local(core, latents):
    frames, rows, cols, channels = latents.shape
    edge = jax.ShapeDtypeStruct((frames, 1, cols, channels), jnp.bfloat16)
    return pl.pallas_call(
        local_kernel,
        out_shape=(
            jax.ShapeDtypeStruct((2, channels), jnp.float32),
            edge,
            edge,
            jax.ShapeDtypeStruct((frames * (rows + 2) * cols + 16, channels), jnp.bfloat16),
        ),
        in_specs=[scalars, whole],
        out_specs=(whole,) * 4,
        compiler_params=params(2),
    )(core, latents)


def merge(parts, entries):
    mean = sum(part[0] for part in parts) / len(parts)
    apart = sum((part[0] - mean) ** 2 for part in parts) * entries
    return jnp.stack([mean, sum(part[1] for part in parts) + apart])


def pack_kernel(frames, rows, cols, edge_ref, stats_ref, sibling_ref, facing_ref, _, out_ref):
    count = frames * rows * cols
    for f in range(frames):
        first = f * rows * cols
        last = first + (rows - 1) * cols
        for start, edge, mirror in ((first, 0, first + 2 * cols), (last, 1, last - 2 * cols)):
            @pl.when(edge_ref[edge] == 0)
            def _():
                out_ref[start : start + cols, :] = sibling_ref[f, 0]

            @pl.when(edge_ref[edge] == 1)
            def _():
                out_ref[start : start + cols, :] = facing_ref[f, 0]

            @pl.when(edge_ref[edge] == 2)
            def _():
                out_ref[start : start + cols, :] = out_ref[mirror : mirror + cols, :]

    rest = stats_ref[...]
    terms = []
    for _ in range(3):
        term = rest.astype(jnp.bfloat16).astype(jnp.float32)
        terms.append(term)
        rest = rest - term
    unused = out_ref.shape[0] - count - 6
    terms.append(jnp.zeros((unused, rest.shape[1]), jnp.float32))
    out_ref[count:, :] = jnp.concatenate(terms, axis=0).astype(jnp.bfloat16)


def pack(edges, stats, sibling, facing, payload, frames, rows, cols):
    return pl.pallas_call(
        functools.partial(pack_kernel, frames, rows, cols),
        out_shape=jax.ShapeDtypeStruct(payload.shape, jnp.bfloat16),
        in_specs=[scalars] + [whole] * 4,
        out_specs=whole,
        input_output_aliases={4: 0},
        compiler_params=params(2),
    )(edges, stats, sibling, facing, payload)


def held_kernel(in_ref, out_ref):
    pass


def hold(block):
    return pl.pallas_call(
        held_kernel,
        out_shape=jax.ShapeDtypeStruct(block.shape, block.dtype),
        in_specs=[whole],
        out_specs=whole,
        input_output_aliases={0: 0},
        compiler_params=params(1),
        cost_estimate=pl.CostEstimate(flops=10**10, bytes_accessed=0, transcendentals=0),
    )(block)


def pick_kernel(which_ref, one_ref, other_ref, out_ref):
    @pl.when(which_ref[0] != 0)
    def _():
        out_ref[...] = one_ref[...]

    @pl.when(which_ref[0] == 0)
    def _():
        out_ref[...] = other_ref[...]


def pick(which, one, other):
    return pl.pallas_call(
        pick_kernel,
        out_shape=jax.ShapeDtypeStruct(one.shape, one.dtype),
        in_specs=[scalars] + [whole] * 2,
        out_specs=whole,
        compiler_params=params(2),
        cost_estimate=pl.CostEstimate(flops=0, bytes_accessed=one.size, transcendentals=0),
    )(which, one, other)


def lane_group_sum(x, size):
    lane = lax.broadcasted_iota(jnp.int32, x.shape, 1)
    step = 1
    while step < size:
        up = pltpu.roll(x, x.shape[1] - step, 1)
        down = pltpu.roll(x, step, 1)
        x = x + jnp.where((lane & step) == 0, up, down)
        step *= 2
    return x


def activate_kernel(held, rows, entries, place_ref, affine_ref, *refs):
    *piece_refs, even_ref, odd_ref, scratch, norm = refs
    channels = piece_refs[0].shape[1]
    frames = held * len(piece_refs)
    cols = odd_ref.shape[1] // frames
    tail = held * rows * cols
    size = channels // GROUPS

    def norms(lanes):
        means, squares = [], []
        for piece_ref in piece_refs:
            terms = piece_ref[tail : tail + 16, lanes].astype(jnp.float32)
            both = terms[0:2] + terms[2:4] + terms[4:6]
            means.append(both[0:1])
            squares.append(both[1:2])
        count = len(piece_refs) * size
        mean = lane_group_sum(jnp.broadcast_to(sum(means), (8, LANES)), size) / count
        spread = sum(squares) + entries * sum((m - mean[0:1]) ** 2 for m in means)
        var = lane_group_sum(jnp.broadcast_to(spread, (8, LANES)), size) / (count * entries)
        norm[0:1, lanes] = mean[0:1]
        norm[1:2, lanes] = lax.rsqrt(var[0:1] + epsilon) * affine_ref[0:1, lanes]
        norm[2:3, lanes] = affine_ref[1:2, lanes]

    blocks = channels // LANES
    for block in range(blocks):
        norms(pl.ds(block * LANES, LANES))
    last = (cols + 1) * frames

    def step(index, carry):
        pair, block = index // blocks, index % blocks
        lanes = pl.ds(pl.multiple_of(block * LANES, LANES), LANES)
        mean, scale, bias = norm[0:1, lanes], norm[1:2, lanes], norm[2:3, lanes]
        for p, piece_ref in enumerate(piece_refs):
            for f in range(held):
                start = pl.multiple_of((f * rows + 2 * pair) * cols, 16)
                x = piece_ref[pl.ds(start, 2 * cols), lanes].astype(jnp.float32)
                h = 0.5 * ((x - mean) * scale + bias)
                h = h + h * jnp.tanh(h)
                for r in range(2):
                    scratch[r, pl.ds(frames + place_ref[p] + f, cols, stride=frames), :] = h[r * cols : (r + 1) * cols]
        for r in range(2):
            scratch[r, 0:frames, :] = scratch[r, 2 * frames : 3 * frames, :]
            scratch[r, last : last + frames, :] = scratch[r, last - 2 * frames : last - frames, :]
            even_ref[2 * pair + r, :, lanes] = scratch[r].astype(jnp.bfloat16)
            odd_ref[2 * pair + r, :, lanes] = scratch[r, frames:last, :].astype(jnp.bfloat16)
        return carry

    lax.fori_loop(0, rows // 2 * blocks, step, 0)


def activate(places, affine, pieces, held, rows, cols, entries):
    channels = pieces[0].shape[1]
    frames = held * len(pieces)
    return pl.pallas_call(
        functools.partial(activate_kernel, held, rows, entries),
        out_shape=(
            jax.ShapeDtypeStruct((rows, (cols + 2) * frames, channels), jnp.bfloat16),
            jax.ShapeDtypeStruct((rows, cols * frames, channels), jnp.bfloat16),
        ),
        in_specs=[scalars, whole] + [whole] * len(pieces),
        out_specs=(whole, whole),
        scratch_shapes=[
            pltpu.VMEM((2, (cols + 2) * frames, LANES), jnp.float32),
            pltpu.VMEM((3, channels), jnp.float32),
        ],
        compiler_params=params(4),
        cost_estimate=pl.CostEstimate(
            flops=10 * frames * rows * cols * channels,
            bytes_accessed=6 * frames * rows * cols * channels,
            transcendentals=frames * rows * cols * channels,
        ),
    )(places, affine, *pieces)


def conv_kernel(count, with_other, place_ref, slot_ref, half_ref, even_ref, odd_ref, bias_ref, *refs):
    piece_refs, refs = refs[:count], refs[count:]
    if with_other:
        other_ref, refs = refs[0], refs[1:]
    out_refs, (taps, sums, placed) = refs[:-3], refs[-3:]
    rows = even_ref.shape[0] - 2
    per_row = odd_ref.shape[1]
    frames = placed.shape[0]
    cols = per_row // frames
    channels = even_ref.shape[2]
    width = taps.shape[2] * taps.shape[3]
    for p, piece_ref in enumerate(piece_refs):
        slot = slot_ref[p]
        for tap in range(27):
            taps[tap % 9, tap // 9, slot] = piece_ref[tap]

    for y in range(rows):
        total = None
        for tap in range(9):
            b, c = tap // 3, tap % 3
            if c == 1:
                window = odd_ref[y + b]
            else:
                window = even_ref[y + b, pl.ds(c * frames, per_row), :]
            product = lax.dot_general(
                window,
                taps[tap].reshape(3 * width, channels),
                (((1,), (1,)), ((), ())),
                preferred_element_type=jnp.float32,
            )
            total = product if total is None else total + product
        place = slice(y * per_row, (y + 1) * per_row)
        sums[0, place, :] = total[:, : 2 * width]
        sums[1, place, 0:width] = total[:, 2 * width :]

    count = rows * cols
    lane = lax.broadcasted_iota(jnp.int32, (count, 2 * width), 1)
    low = lane < width
    for f in range(frames):
        value = sums[1, pl.ds(f, count, stride=frames), :]
        if f >= 1:
            value = value + pltpu.roll(sums[0, pl.ds(f - 1, count, stride=frames), :], width, 1)
        if f >= 2:
            value = value + sums[0, pl.ds(f - 2, count, stride=frames), :]
        value = jnp.where(low, value, pltpu.roll(value, width, 1)) + bias_ref[...]
        if with_other:
            value = jnp.where(low == (half_ref[0] == 0), value, other_ref[f].astype(jnp.float32))
        placed[f] = value.astype(jnp.bfloat16)
    if with_other:
        for p, out_ref in enumerate(out_refs):
            out_ref[...] = placed[pl.ds(place_ref[p], out_ref.shape[0])]
    else:
        out_refs[0][...] = placed[...]


def convolve(places, slots, half, even, odd, bias, pieces, frames, other=None):
    rows, per_row, channels = even.shape[0] - 2, odd.shape[1], even.shape[2]
    positions = rows * per_row // frames
    each = pieces[0].shape[1]
    width = each * len(pieces)
    if other is None:
        shapes, others = [(frames, positions, 2 * width)], []
    else:
        groups = places.shape[0]
        shapes, others = [(frames // groups, positions, 2 * width)] * groups, [other]
    return pl.pallas_call(
        functools.partial(conv_kernel, len(pieces), other is not None),
        out_shape=tuple(jax.ShapeDtypeStruct(shape, jnp.bfloat16) for shape in shapes),
        in_specs=[scalars] * 3 + [whole] * (3 + len(pieces) + len(others)),
        out_specs=tuple(whole for _ in shapes),
        scratch_shapes=[
            pltpu.VMEM((9, 3, len(pieces), each, channels), jnp.bfloat16),
            pltpu.VMEM((2, rows * per_row, 2 * width), jnp.float32),
            pltpu.VMEM((frames, positions, 2 * width), jnp.bfloat16),
        ],
        compiler_params=params(10),
        cost_estimate=pl.CostEstimate(
            flops=2 * rows * per_row * channels * width,
            bytes_accessed=2 * channels * width,
            transcendentals=0,
        ),
    )(places, slots, half, even, odd, bias, *pieces, *others)


def place_kernel(place_ref, *refs):
    *piece_refs, out_ref = refs
    width = piece_refs[0].shape[2]
    for p, piece_ref in enumerate(piece_refs):
        start = pl.multiple_of(place_ref[p] * width, LANES)
        out_ref[:, :, pl.ds(start, width)] = piece_ref[...]


def place(groups, pieces):
    held, positions, width = pieces[0].shape
    return pl.pallas_call(
        place_kernel,
        out_shape=jax.ShapeDtypeStruct((held, positions, width * len(pieces)), jnp.bfloat16),
        in_specs=[scalars] + [whole] * len(pieces),
        out_specs=whole,
        compiler_params=params(2),
    )(groups, *pieces)


def body(latents, norm_gain, norm_bias, conv_weight, conv_bias):
    held, row_count, col_count, channels = latents.shape
    group_count = lax.axis_size("frames")
    strips = lax.axis_size("rows")
    group = lax.axis_index("frames")
    strip = lax.axis_index("rows")
    is_line = strips == 4 * CORES
    weight = conv_weight.transpose(0, 1, 2, 4, 3)
    weight = weight.reshape((-1,) + weight.shape[3:])

    core = strip % CORES
    stats, inner, outer, payload = local(core[None], latents)
    sibling = lax.ppermute(inner, "rows", flip("rows", 1))
    facing = [(i, i + 1) for i in range(1, strips - 1, CORES)]
    facing = lax.ppermute(outer, "rows", facing + [(b, a) for a, b in facing])

    width = channels // group_count
    bias = lax.dynamic_slice_in_dim(conv_bias, group * width, width)[None]
    entries = held * row_count * col_count
    if is_line:
        weight = after(weight, sibling, facing)
        first, second = exchange(weight, "rows", [CORES, 2 * CORES])
        chips = range(CORES, strips, CORES)
        stats = merge([stats] + exchange(stats, "rows", chips), entries)
        stats = merge([stats] + exchange(stats, "rows", [1]), 4 * entries)
        entries *= strips
    else:
        distance = 1
        while distance < strips:
            stats = merge([stats] + exchange(stats, "rows", [distance]), entries)
            entries *= 2
            distance *= 2

    if is_line:
        weight, first, second = lax.optimization_barrier((weight, first, second))
        second = hold(second)
        ends = chip_pairs([(1, 0), (2, 3)])
        middle = chip_pairs([(1, 2), (2, 1)])
        third_ends = lax.ppermute(second, "rows", ends)
        third_middle = lax.ppermute(weight, "rows", middle)

    above = jnp.where(strip == 0, 2, 1 - core)
    below = jnp.where(strip == strips - 1, 2, core)
    edges = jnp.stack([above, below]).astype(jnp.int32)
    payload = pack(edges, stats, sibling, facing, payload, held, row_count + 2, col_count)
    strip_pieces = [payload] + exchange(payload, "frames", range(1, group_count))
    groups = jnp.stack([group ^ d for d in range(group_count)]).astype(jnp.int32)
    affine = jnp.stack([norm_gain, norm_bias])
    if is_line:
        near, strip_pieces, far = lax.optimization_barrier(([weight, first], strip_pieces, [second]))
    even, odd = activate(
        groups * held, affine, strip_pieces, held, row_count + 2, col_count, entries
    )

    if is_line:
        near += [lax.ppermute(piece, "rows", flip("rows", 1)) for piece in near]
        slots = jnp.stack([strip, strip ^ 2, strip ^ 1, strip ^ 3]) % 4
        half, other_half = (strip // 4)[None], 1 - (strip // 4)[None]
    else:
        gathered = lax.all_gather(weight, "rows", axis=1, tiled=True)
        near, far = [gathered[:, : width // 2]], [gathered[:, width // 2 :]]
        slots = jnp.zeros((1,), jnp.int32)
        half, other_half = slots, slots + 1
    convolved = functools.partial(
        convolve, groups * held, slots, even=even, odd=odd, frames=held * group_count
    )
    done = convolved(half, bias=bias, pieces=near)[0]
    if is_line:
        third_ends, third_middle, done = lax.optimization_barrier((third_ends, third_middle, done))
        chip = strip // CORES
        at_end = ((chip == 0) | (chip == 3)).astype(jnp.int32)[None]
        third = pick(at_end, third_ends, third_middle)
        far.append(third)
        far += [lax.ppermute(piece, "rows", flip("rows", 1)) for piece in far]
    parts = convolved(other_half, bias=bias, pieces=far, other=done)
    parts = [parts[0]] + [
        lax.ppermute(parts[d], "frames", flip("frames", d)) for d in range(1, group_count)
    ]
    return place(groups, parts).reshape(latents.shape)


def solution(mesh):
    placed = (
        P("frames", "rows", None, None),
        P(),
        P(),
        P(None, None, None, None, ("frames", "rows")),
        P(),
    )
    return jax.shard_map(
        body, mesh=mesh, in_specs=placed, out_specs=P("frames", "rows", None, None), check_vma=False
    )
```

```python
import functools

import jax
import jax.numpy as jnp
from jax import lax
from jax.experimental import pallas as pl
from jax.experimental.pallas import tpu as pltpu
from jax.sharding import PartitionSpec as P

GROUPS = 32
LANES = 128
CORES = 2

epsilon = 1e-06

whole = pl.BlockSpec(memory_space=pltpu.VMEM)
scalars = pl.BlockSpec(memory_space=pltpu.SMEM)


def params(mib):
    return pltpu.CompilerParams(vmem_limit_bytes=mib * 2**20)


def flip(axis, distance):
    return [(i, i ^ distance) for i in range(lax.axis_size(axis))]


def exchange(block, axis, distances):
    return [lax.ppermute(block, axis, flip(axis, d)) for d in distances]


def chip_pairs(pairs):
    return [(CORES * a + c, CORES * b + c) for a, b in pairs for c in range(CORES)]


def after(block, *others):
    return lax.optimization_barrier((block, *others))[0]


def local_kernel(core_ref, x_ref, stats_ref, inner_ref, outer_ref, payload_ref):
    frames, rows, cols, channels = x_ref.shape
    entries = frames * rows * cols
    inner = (rows - 1) * (1 - core_ref[0])
    inner_ref[...] = x_ref[:, pl.ds(inner, 1)]
    outer_ref[...] = x_ref[:, pl.ds(rows - 1 - inner, 1)]
    for f in range(frames):
        start = (f * (rows + 2) + 1) * cols
        payload_ref[start : start + rows * cols, :] = x_ref[f].reshape(rows * cols, channels)
    for block in range(channels // LANES):
        lanes = pl.ds(block * LANES, LANES)
        total = jnp.zeros((8, LANES), jnp.float32)
        for f in range(frames):
            for r in range(rows):
                x = x_ref[f, r, :, lanes].astype(jnp.float32)
                total = total + jnp.sum(x.reshape(-1, 8, LANES), axis=0)
        mean = jnp.sum(total, axis=0, keepdims=True) / entries
        total = jnp.zeros((8, LANES), jnp.float32)
        for f in range(frames):
            for r in range(rows):
                x = x_ref[f, r, :, lanes].astype(jnp.float32) - mean
                total = total + jnp.sum((x * x).reshape(-1, 8, LANES), axis=0)
        stats_ref[0:1, lanes] = mean
        stats_ref[1:2, lanes] = jnp.sum(total, axis=0, keepdims=True)


def local(core, latents):
    frames, rows, cols, channels = latents.shape
    edge = jax.ShapeDtypeStruct((frames, 1, cols, channels), jnp.bfloat16)
    return pl.pallas_call(
        local_kernel,
        out_shape=(
            jax.ShapeDtypeStruct((2, channels), jnp.float32),
            edge,
            edge,
            jax.ShapeDtypeStruct((frames * (rows + 2) * cols + 16, channels), jnp.bfloat16),
        ),
        in_specs=[scalars, whole],
        out_specs=(whole,) * 4,
        compiler_params=params(2),
    )(core, latents)


def merge(parts, entries):
    mean = sum(part[0] for part in parts) / len(parts)
    apart = sum((part[0] - mean) ** 2 for part in parts) * entries
    return jnp.stack([mean, sum(part[1] for part in parts) + apart])


def pack_kernel(frames, rows, cols, edge_ref, stats_ref, sibling_ref, facing_ref, _, out_ref):
    count = frames * rows * cols
    for f in range(frames):
        first = f * rows * cols
        last = first + (rows - 1) * cols
        for start, edge, mirror in ((first, 0, first + 2 * cols), (last, 1, last - 2 * cols)):
            @pl.when(edge_ref[edge] == 0)
            def _():
                out_ref[start : start + cols, :] = sibling_ref[f, 0]

            @pl.when(edge_ref[edge] == 1)
            def _():
                out_ref[start : start + cols, :] = facing_ref[f, 0]

            @pl.when(edge_ref[edge] == 2)
            def _():
                out_ref[start : start + cols, :] = out_ref[mirror : mirror + cols, :]

    rest = stats_ref[...]
    terms = []
    for _ in range(3):
        term = rest.astype(jnp.bfloat16).astype(jnp.float32)
        terms.append(term)
        rest = rest - term
    unused = out_ref.shape[0] - count - 6
    terms.append(jnp.zeros((unused, rest.shape[1]), jnp.float32))
    out_ref[count:, :] = jnp.concatenate(terms, axis=0).astype(jnp.bfloat16)


def pack(edges, stats, sibling, facing, payload, frames, rows, cols):
    return pl.pallas_call(
        functools.partial(pack_kernel, frames, rows, cols),
        out_shape=jax.ShapeDtypeStruct(payload.shape, jnp.bfloat16),
        in_specs=[scalars] + [whole] * 4,
        out_specs=whole,
        input_output_aliases={4: 0},
        compiler_params=params(2),
    )(edges, stats, sibling, facing, payload)


def held_kernel(in_ref, out_ref):
    pass


def hold(block):
    return pl.pallas_call(
        held_kernel,
        out_shape=jax.ShapeDtypeStruct(block.shape, block.dtype),
        in_specs=[whole],
        out_specs=whole,
        input_output_aliases={0: 0},
        compiler_params=params(1),
        cost_estimate=pl.CostEstimate(flops=10**10, bytes_accessed=0, transcendentals=0),
    )(block)


def pick_kernel(which_ref, one_ref, other_ref, out_ref):
    @pl.when(which_ref[0] != 0)
    def _():
        out_ref[...] = one_ref[...]

    @pl.when(which_ref[0] == 0)
    def _():
        out_ref[...] = other_ref[...]


def pick(which, one, other):
    return pl.pallas_call(
        pick_kernel,
        out_shape=jax.ShapeDtypeStruct(one.shape, one.dtype),
        in_specs=[scalars] + [whole] * 2,
        out_specs=whole,
        compiler_params=params(2),
        cost_estimate=pl.CostEstimate(flops=0, bytes_accessed=one.size, transcendentals=0),
    )(which, one, other)


def lane_group_sum(x, size):
    lane = lax.broadcasted_iota(jnp.int32, x.shape, 1)
    step = 1
    while step < size:
        up = pltpu.roll(x, x.shape[1] - step, 1)
        down = pltpu.roll(x, step, 1)
        x = x + jnp.where((lane & step) == 0, up, down)
        step *= 2
    return x


def activate_kernel(held, rows, entries, place_ref, affine_ref, *refs):
    *piece_refs, even_ref, odd_ref, scratch, norm = refs
    channels = piece_refs[0].shape[1]
    frames = held * len(piece_refs)
    cols = odd_ref.shape[1] // frames
    tail = held * rows * cols
    size = channels // GROUPS

    def norms(lanes):
        means, squares = [], []
        for piece_ref in piece_refs:
            terms = piece_ref[tail : tail + 16, lanes].astype(jnp.float32)
            both = terms[0:2] + terms[2:4] + terms[4:6]
            means.append(both[0:1])
            squares.append(both[1:2])
        count = len(piece_refs) * size
        mean = lane_group_sum(jnp.broadcast_to(sum(means), (8, LANES)), size) / count
        spread = sum(squares) + entries * sum((m - mean[0:1]) ** 2 for m in means)
        var = lane_group_sum(jnp.broadcast_to(spread, (8, LANES)), size) / (count * entries)
        norm[0:1, lanes] = mean[0:1]
        norm[1:2, lanes] = lax.rsqrt(var[0:1] + epsilon) * affine_ref[0:1, lanes]
        norm[2:3, lanes] = affine_ref[1:2, lanes]

    blocks = channels // LANES
    for block in range(blocks):
        norms(pl.ds(block * LANES, LANES))
    last = (cols + 1) * frames

    def step(index, carry):
        pair, block = index // blocks, index % blocks
        lanes = pl.ds(pl.multiple_of(block * LANES, LANES), LANES)
        mean, scale, bias = norm[0:1, lanes], norm[1:2, lanes], norm[2:3, lanes]
        for p, piece_ref in enumerate(piece_refs):
            for f in range(held):
                start = pl.multiple_of((f * rows + 2 * pair) * cols, 16)
                x = piece_ref[pl.ds(start, 2 * cols), lanes].astype(jnp.float32)
                h = 0.5 * ((x - mean) * scale + bias)
                h = h + h * jnp.tanh(h)
                for r in range(2):
                    scratch[r, pl.ds(frames + place_ref[p] + f, cols, stride=frames), :] = h[r * cols : (r + 1) * cols]
        for r in range(2):
            scratch[r, 0:frames, :] = scratch[r, 2 * frames : 3 * frames, :]
            scratch[r, last : last + frames, :] = scratch[r, last - 2 * frames : last - frames, :]
            even_ref[2 * pair + r, :, lanes] = scratch[r].astype(jnp.bfloat16)
            odd_ref[2 * pair + r, :, lanes] = scratch[r, frames:last, :].astype(jnp.bfloat16)
        return carry

    lax.fori_loop(0, rows // 2 * blocks, step, 0)


def activate(places, affine, pieces, held, rows, cols, entries):
    channels = pieces[0].shape[1]
    frames = held * len(pieces)
    return pl.pallas_call(
        functools.partial(activate_kernel, held, rows, entries),
        out_shape=(
            jax.ShapeDtypeStruct((rows, (cols + 2) * frames, channels), jnp.bfloat16),
            jax.ShapeDtypeStruct((rows, cols * frames, channels), jnp.bfloat16),
        ),
        in_specs=[scalars, whole] + [whole] * len(pieces),
        out_specs=(whole, whole),
        scratch_shapes=[
            pltpu.VMEM((2, (cols + 2) * frames, LANES), jnp.float32),
            pltpu.VMEM((3, channels), jnp.float32),
        ],
        compiler_params=params(4),
        cost_estimate=pl.CostEstimate(
            flops=10 * frames * rows * cols * channels,
            bytes_accessed=6 * frames * rows * cols * channels,
            transcendentals=frames * rows * cols * channels,
        ),
    )(places, affine, *pieces)


def conv_kernel(count, with_other, place_ref, slot_ref, half_ref, even_ref, odd_ref, bias_ref, *refs):
    piece_refs, refs = refs[:count], refs[count:]
    if with_other:
        other_ref, refs = refs[0], refs[1:]
    out_refs, (taps, sums, placed) = refs[:-3], refs[-3:]
    rows = even_ref.shape[0] - 2
    per_row = odd_ref.shape[1]
    frames = placed.shape[0]
    cols = per_row // frames
    channels = even_ref.shape[2]
    width = taps.shape[2] * taps.shape[3]
    for p, piece_ref in enumerate(piece_refs):
        slot = slot_ref[p]
        for tap in range(27):
            taps[tap % 9, tap // 9, slot] = piece_ref[tap]

    for y in range(rows):
        total = None
        for tap in range(9):
            b, c = tap // 3, tap % 3
            if c == 1:
                window = odd_ref[y + b]
            else:
                window = even_ref[y + b, pl.ds(c * frames, per_row), :]
            product = lax.dot_general(
                window,
                taps[tap].reshape(3 * width, channels),
                (((1,), (1,)), ((), ())),
                preferred_element_type=jnp.float32,
            )
            total = product if total is None else total + product
        place = slice(y * per_row, (y + 1) * per_row)
        sums[0, place, :] = total[:, : 2 * width]
        sums[1, place, 0:width] = total[:, 2 * width :]

    count = rows * cols
    lane = lax.broadcasted_iota(jnp.int32, (count, 2 * width), 1)
    low = lane < width
    for f in range(frames):
        value = sums[1, pl.ds(f, count, stride=frames), :]
        if f >= 1:
            value = value + pltpu.roll(sums[0, pl.ds(f - 1, count, stride=frames), :], width, 1)
        if f >= 2:
            value = value + sums[0, pl.ds(f - 2, count, stride=frames), :]
        value = jnp.where(low, value, pltpu.roll(value, width, 1)) + bias_ref[...]
        if with_other:
            value = jnp.where(low == (half_ref[0] == 0), value, other_ref[f].astype(jnp.float32))
        placed[f] = value.astype(jnp.bfloat16)
    if with_other:
        for p, out_ref in enumerate(out_refs):
            out_ref[...] = placed[pl.ds(place_ref[p], out_ref.shape[0])]
    else:
        out_refs[0][...] = placed[...]


def convolve(places, slots, half, even, odd, bias, pieces, frames, other=None):
    rows, per_row, channels = even.shape[0] - 2, odd.shape[1], even.shape[2]
    positions = rows * per_row // frames
    each = pieces[0].shape[1]
    width = each * len(pieces)
    if other is None:
        shapes, others = [(frames, positions, 2 * width)], []
    else:
        groups = places.shape[0]
        shapes, others = [(frames // groups, positions, 2 * width)] * groups, [other]
    return pl.pallas_call(
        functools.partial(conv_kernel, len(pieces), other is not None),
        out_shape=tuple(jax.ShapeDtypeStruct(shape, jnp.bfloat16) for shape in shapes),
        in_specs=[scalars] * 3 + [whole] * (3 + len(pieces) + len(others)),
        out_specs=tuple(whole for _ in shapes),
        scratch_shapes=[
            pltpu.VMEM((9, 3, len(pieces), each, channels), jnp.bfloat16),
            pltpu.VMEM((2, rows * per_row, 2 * width), jnp.float32),
            pltpu.VMEM((frames, positions, 2 * width), jnp.bfloat16),
        ],
        compiler_params=params(10),
        cost_estimate=pl.CostEstimate(
            flops=2 * rows * per_row * channels * width,
            bytes_accessed=2 * channels * width,
            transcendentals=0,
        ),
    )(places, slots, half, even, odd, bias, *pieces, *others)


def place_kernel(place_ref, *refs):
    *piece_refs, out_ref = refs
    width = piece_refs[0].shape[2]
    for p, piece_ref in enumerate(piece_refs):
        start = pl.multiple_of(place_ref[p] * width, LANES)
        out_ref[:, :, pl.ds(start, width)] = piece_ref[...]


def place(groups, pieces):
    held, positions, width = pieces[0].shape
    return pl.pallas_call(
        place_kernel,
        out_shape=jax.ShapeDtypeStruct((held, positions, width * len(pieces)), jnp.bfloat16),
        in_specs=[scalars] + [whole] * len(pieces),
        out_specs=whole,
        compiler_params=params(2),
    )(groups, *pieces)


def body(latents, norm_gain, norm_bias, conv_weight, conv_bias):
    held, row_count, col_count, channels = latents.shape
    group_count = lax.axis_size("frames")
    strips = lax.axis_size("rows")
    group = lax.axis_index("frames")
    strip = lax.axis_index("rows")
    is_line = strips == 4 * CORES
    weight = conv_weight.transpose(0, 1, 2, 4, 3)
    weight = weight.reshape((-1,) + weight.shape[3:])

    core = strip % CORES
    stats, inner, outer, payload = local(core[None], latents)
    sibling = lax.ppermute(inner, "rows", flip("rows", 1))
    facing = [(i, i + 1) for i in range(1, strips - 1, CORES)]
    facing = lax.ppermute(outer, "rows", facing + [(b, a) for a, b in facing])

    width = channels // group_count
    bias = lax.dynamic_slice_in_dim(conv_bias, group * width, width)[None]
    entries = held * row_count * col_count
    if is_line:
        weight = after(weight, sibling, facing)
        first, second = exchange(weight, "rows", [CORES, 2 * CORES])
        for distance in (1, CORES, 2 * CORES):
            stats = merge([stats] + exchange(stats, "rows", [distance]), entries)
            entries *= 2
    else:
        distance = 1
        while distance < strips:
            stats = merge([stats] + exchange(stats, "rows", [distance]), entries)
            entries *= 2
            distance *= 2

    if is_line:
        weight, first, second = lax.optimization_barrier((weight, first, second))
        second = hold(second)
        ends = chip_pairs([(1, 0), (2, 3)])
        middle = chip_pairs([(1, 2), (2, 1)])
        third_ends = lax.ppermute(second, "rows", ends)
        third_middle = lax.ppermute(weight, "rows", middle)

    above = jnp.where(strip == 0, 2, 1 - core)
    below = jnp.where(strip == strips - 1, 2, core)
    edges = jnp.stack([above, below]).astype(jnp.int32)
    payload = pack(edges, stats, sibling, facing, payload, held, row_count + 2, col_count)
    distances = [0] + list(reversed(range(1, group_count)))
    strip_pieces = [payload] + exchange(payload, "frames", distances[1:])
    groups = jnp.stack([group ^ d for d in range(group_count)]).astype(jnp.int32)
    affine = jnp.stack([norm_gain, norm_bias])
    if is_line:
        near, strip_pieces, far = lax.optimization_barrier(([weight, first], strip_pieces, [second]))
    places = jnp.stack([group ^ d for d in distances]).astype(jnp.int32) * held
    even, odd = activate(
        places, affine, strip_pieces, held, row_count + 2, col_count, entries
    )

    if is_line:
        near += [lax.ppermute(piece, "rows", flip("rows", 1)) for piece in near]
        slots = jnp.stack([strip, strip ^ 2, strip ^ 1, strip ^ 3]) % 4
        half, other_half = (strip // 4)[None], 1 - (strip // 4)[None]
    else:
        gathered = lax.all_gather(weight, "rows", axis=1, tiled=True)
        near, far = [gathered[:, : width // 2]], [gathered[:, width // 2 :]]
        slots = jnp.zeros((1,), jnp.int32)
        half, other_half = slots, slots + 1
    convolved = functools.partial(
        convolve, groups * held, slots, even=even, odd=odd, frames=held * group_count
    )
    done = convolved(half, bias=bias, pieces=near)[0]
    if is_line:
        third_ends, third_middle, done = lax.optimization_barrier((third_ends, third_middle, done))
        chip = strip // CORES
        at_end = ((chip == 0) | (chip == 3)).astype(jnp.int32)[None]
        third = pick(at_end, third_ends, third_middle)
        far.append(third)
        far += [lax.ppermute(piece, "rows", flip("rows", 1)) for piece in far]
    parts = convolved(other_half, bias=bias, pieces=far, other=done)
    parts = [parts[0]] + [
        lax.ppermute(parts[d], "frames", flip("frames", d)) for d in range(1, group_count)
    ]
    return place(groups, parts).reshape(latents.shape)


def solution(mesh):
    placed = (
        P("frames", "rows", None, None),
        P(),
        P(),
        P(None, None, None, None, ("frames", "rows")),
        P(),
    )
    return jax.shard_map(
        body, mesh=mesh, in_specs=placed, out_specs=P("frames", "rows", None, None), check_vma=False
    )
```

```python
import functools

import jax
import jax.numpy as jnp
from jax import lax
from jax.experimental import pallas as pl
from jax.experimental.pallas import tpu as pltpu
from jax.sharding import PartitionSpec as P

GROUPS = 32
LANES = 128
CORES = 2

epsilon = 1e-06

whole = pl.BlockSpec(memory_space=pltpu.VMEM)
scalars = pl.BlockSpec(memory_space=pltpu.SMEM)


def params(mib):
    return pltpu.CompilerParams(vmem_limit_bytes=mib * 2**20)


def flip(axis, distance):
    return [(i, i ^ distance) for i in range(lax.axis_size(axis))]


def exchange(block, axis, distances):
    return [lax.ppermute(block, axis, flip(axis, d)) for d in distances]


def chip_pairs(pairs):
    return [(CORES * a + c, CORES * b + c) for a, b in pairs for c in range(CORES)]


def after(block, *others):
    return lax.optimization_barrier((block, *others))[0]


def local_kernel(core_ref, x_ref, stats_ref, inner_ref, outer_ref, payload_ref):
    frames, rows, cols, channels = x_ref.shape
    entries = frames * rows * cols
    inner = (rows - 1) * (1 - core_ref[0])
    inner_ref[...] = x_ref[:, pl.ds(inner, 1)]
    outer_ref[...] = x_ref[:, pl.ds(rows - 1 - inner, 1)]
    for f in range(frames):
        start = (f * (rows + 2) + 1) * cols
        payload_ref[start : start + rows * cols, :] = x_ref[f].reshape(rows * cols, channels)
    for block in range(channels // LANES):
        lanes = pl.ds(block * LANES, LANES)
        total = jnp.zeros((8, LANES), jnp.float32)
        for f in range(frames):
            for r in range(rows):
                x = x_ref[f, r, :, lanes].astype(jnp.float32)
                total = total + jnp.sum(x.reshape(-1, 8, LANES), axis=0)
        mean = jnp.sum(total, axis=0, keepdims=True) / entries
        total = jnp.zeros((8, LANES), jnp.float32)
        for f in range(frames):
            for r in range(rows):
                x = x_ref[f, r, :, lanes].astype(jnp.float32) - mean
                total = total + jnp.sum((x * x).reshape(-1, 8, LANES), axis=0)
        stats_ref[0:1, lanes] = mean
        stats_ref[1:2, lanes] = jnp.sum(total, axis=0, keepdims=True)


def local(core, latents):
    frames, rows, cols, channels = latents.shape
    edge = jax.ShapeDtypeStruct((frames, 1, cols, channels), jnp.bfloat16)
    return pl.pallas_call(
        local_kernel,
        out_shape=(
            jax.ShapeDtypeStruct((2, channels), jnp.float32),
            edge,
            edge,
            jax.ShapeDtypeStruct((frames * (rows + 2) * cols + 16, channels), jnp.bfloat16),
        ),
        in_specs=[scalars, whole],
        out_specs=(whole,) * 4,
        compiler_params=params(2),
    )(core, latents)


def merge(parts, entries):
    mean = sum(part[0] for part in parts) / len(parts)
    apart = sum((part[0] - mean) ** 2 for part in parts) * entries
    return jnp.stack([mean, sum(part[1] for part in parts) + apart])


def pack_kernel(frames, rows, cols, edge_ref, stats_ref, sibling_ref, facing_ref, _, out_ref):
    count = frames * rows * cols
    for f in range(frames):
        first = f * rows * cols
        last = first + (rows - 1) * cols
        for start, edge, mirror in ((first, 0, first + 2 * cols), (last, 1, last - 2 * cols)):
            @pl.when(edge_ref[edge] == 0)
            def _():
                out_ref[start : start + cols, :] = sibling_ref[f, 0]

            @pl.when(edge_ref[edge] == 1)
            def _():
                out_ref[start : start + cols, :] = facing_ref[f, 0]

            @pl.when(edge_ref[edge] == 2)
            def _():
                out_ref[start : start + cols, :] = out_ref[mirror : mirror + cols, :]

    rest = stats_ref[...]
    terms = []
    for _ in range(3):
        term = rest.astype(jnp.bfloat16).astype(jnp.float32)
        terms.append(term)
        rest = rest - term
    unused = out_ref.shape[0] - count - 6
    terms.append(jnp.zeros((unused, rest.shape[1]), jnp.float32))
    out_ref[count:, :] = jnp.concatenate(terms, axis=0).astype(jnp.bfloat16)


def pack(edges, stats, sibling, facing, payload, frames, rows, cols):
    return pl.pallas_call(
        functools.partial(pack_kernel, frames, rows, cols),
        out_shape=jax.ShapeDtypeStruct(payload.shape, jnp.bfloat16),
        in_specs=[scalars] + [whole] * 4,
        out_specs=whole,
        input_output_aliases={4: 0},
        compiler_params=params(2),
    )(edges, stats, sibling, facing, payload)


def held_kernel(in_ref, out_ref):
    pass


def hold(block):
    return pl.pallas_call(
        held_kernel,
        out_shape=jax.ShapeDtypeStruct(block.shape, block.dtype),
        in_specs=[whole],
        out_specs=whole,
        input_output_aliases={0: 0},
        compiler_params=params(1),
        cost_estimate=pl.CostEstimate(flops=10**10, bytes_accessed=0, transcendentals=0),
    )(block)


def pick_kernel(which_ref, one_ref, other_ref, out_ref):
    @pl.when(which_ref[0] != 0)
    def _():
        out_ref[...] = one_ref[...]

    @pl.when(which_ref[0] == 0)
    def _():
        out_ref[...] = other_ref[...]


def pick(which, one, other):
    return pl.pallas_call(
        pick_kernel,
        out_shape=jax.ShapeDtypeStruct(one.shape, one.dtype),
        in_specs=[scalars] + [whole] * 2,
        out_specs=whole,
        compiler_params=params(2),
        cost_estimate=pl.CostEstimate(flops=0, bytes_accessed=one.size, transcendentals=0),
    )(which, one, other)


def lane_group_sum(x, size):
    lane = lax.broadcasted_iota(jnp.int32, x.shape, 1)
    step = 1
    while step < size:
        up = pltpu.roll(x, x.shape[1] - step, 1)
        down = pltpu.roll(x, step, 1)
        x = x + jnp.where((lane & step) == 0, up, down)
        step *= 2
    return x


def activate_kernel(held, rows, entries, place_ref, affine_ref, *refs):
    *piece_refs, even_ref, odd_ref, scratch, norm = refs
    channels = piece_refs[0].shape[1]
    frames = held * len(piece_refs)
    cols = odd_ref.shape[1] // frames
    tail = held * rows * cols
    size = channels // GROUPS

    def norms(lanes):
        means, squares = [], []
        for piece_ref in piece_refs:
            terms = piece_ref[tail : tail + 16, lanes].astype(jnp.float32)
            both = terms[0:2] + terms[2:4] + terms[4:6]
            means.append(both[0:1])
            squares.append(both[1:2])
        count = len(piece_refs) * size
        mean = lane_group_sum(jnp.broadcast_to(sum(means), (8, LANES)), size) / count
        spread = sum(squares) + entries * sum((m - mean[0:1]) ** 2 for m in means)
        var = lane_group_sum(jnp.broadcast_to(spread, (8, LANES)), size) / (count * entries)
        norm[0:1, lanes] = mean[0:1]
        norm[1:2, lanes] = lax.rsqrt(var[0:1] + epsilon) * affine_ref[0:1, lanes]
        norm[2:3, lanes] = affine_ref[1:2, lanes]

    blocks = channels // LANES
    for block in range(blocks):
        norms(pl.ds(block * LANES, LANES))
    last = (cols + 1) * frames

    def step(index, carry):
        pair, block = index // blocks, index % blocks
        lanes = pl.ds(pl.multiple_of(block * LANES, LANES), LANES)
        mean, scale, bias = norm[0:1, lanes], norm[1:2, lanes], norm[2:3, lanes]
        for p, piece_ref in enumerate(piece_refs):
            for f in range(held):
                start = pl.multiple_of((f * rows + 2 * pair) * cols, 16)
                x = piece_ref[pl.ds(start, 2 * cols), lanes].astype(jnp.float32)
                h = 0.5 * ((x - mean) * scale + bias)
                h = h + h * jnp.tanh(h)
                for r in range(2):
                    scratch[r, pl.ds(frames + place_ref[p] + f, cols, stride=frames), :] = h[r * cols : (r + 1) * cols]
        for r in range(2):
            scratch[r, 0:frames, :] = scratch[r, 2 * frames : 3 * frames, :]
            scratch[r, last : last + frames, :] = scratch[r, last - 2 * frames : last - frames, :]
            even_ref[2 * pair + r, :, lanes] = scratch[r].astype(jnp.bfloat16)
            odd_ref[2 * pair + r, :, lanes] = scratch[r, frames:last, :].astype(jnp.bfloat16)
        return carry

    lax.fori_loop(0, rows // 2 * blocks, step, 0)


def activate(places, affine, pieces, held, rows, cols, entries):
    channels = pieces[0].shape[1]
    frames = held * len(pieces)
    return pl.pallas_call(
        functools.partial(activate_kernel, held, rows, entries),
        out_shape=(
            jax.ShapeDtypeStruct((rows, (cols + 2) * frames, channels), jnp.bfloat16),
            jax.ShapeDtypeStruct((rows, cols * frames, channels), jnp.bfloat16),
        ),
        in_specs=[scalars, whole] + [whole] * len(pieces),
        out_specs=(whole, whole),
        scratch_shapes=[
            pltpu.VMEM((2, (cols + 2) * frames, LANES), jnp.float32),
            pltpu.VMEM((3, channels), jnp.float32),
        ],
        compiler_params=params(4),
        cost_estimate=pl.CostEstimate(
            flops=10 * frames * rows * cols * channels,
            bytes_accessed=6 * frames * rows * cols * channels,
            transcendentals=frames * rows * cols * channels,
        ),
    )(places, affine, *pieces)


def conv_kernel(count, with_other, place_ref, slot_ref, half_ref, even_ref, odd_ref, bias_ref, *refs):
    piece_refs, refs = refs[:count], refs[count:]
    if with_other:
        other_ref, refs = refs[0], refs[1:]
    out_refs, (taps, sums, placed) = refs[:-3], refs[-3:]
    rows = even_ref.shape[0] - 2
    per_row = odd_ref.shape[1]
    frames = placed.shape[0]
    cols = per_row // frames
    channels = even_ref.shape[2]
    width = taps.shape[2] * taps.shape[3]
    for p, piece_ref in enumerate(piece_refs):
        slot = slot_ref[p]
        for tap in range(27):
            taps[tap % 9, tap // 9, slot] = piece_ref[tap]

    for y in range(rows):
        total = None
        for tap in range(9):
            b, c = tap // 3, tap % 3
            if c == 1:
                window = odd_ref[y + b]
            else:
                window = even_ref[y + b, pl.ds(c * frames, per_row), :]
            product = lax.dot_general(
                window,
                taps[tap].reshape(3 * width, channels),
                (((1,), (1,)), ((), ())),
                preferred_element_type=jnp.float32,
            )
            total = product if total is None else total + product
        place = slice(y * per_row, (y + 1) * per_row)
        sums[0, place, :] = total[:, : 2 * width]
        sums[1, place, 0:width] = total[:, 2 * width :]

    count = rows * cols
    lane = lax.broadcasted_iota(jnp.int32, (count, 2 * width), 1)
    low = lane < width
    for f in range(frames):
        value = sums[1, pl.ds(f, count, stride=frames), :]
        if f >= 1:
            value = value + pltpu.roll(sums[0, pl.ds(f - 1, count, stride=frames), :], width, 1)
        if f >= 2:
            value = value + sums[0, pl.ds(f - 2, count, stride=frames), :]
        value = jnp.where(low, value, pltpu.roll(value, width, 1)) + bias_ref[...]
        if with_other:
            value = jnp.where(low == (half_ref[0] == 0), value, other_ref[f].astype(jnp.float32))
        placed[f] = value.astype(jnp.bfloat16)
    if with_other:
        for p, out_ref in enumerate(out_refs):
            out_ref[...] = placed[pl.ds(place_ref[p], out_ref.shape[0])]
    else:
        out_refs[0][...] = placed[...]


def convolve(places, slots, half, even, odd, bias, pieces, frames, other=None):
    rows, per_row, channels = even.shape[0] - 2, odd.shape[1], even.shape[2]
    positions = rows * per_row // frames
    each = pieces[0].shape[1]
    width = each * len(pieces)
    if other is None:
        shapes, others = [(frames, positions, 2 * width)], []
    else:
        groups = places.shape[0]
        shapes, others = [(frames // groups, positions, 2 * width)] * groups, [other]
    return pl.pallas_call(
        functools.partial(conv_kernel, len(pieces), other is not None),
        out_shape=tuple(jax.ShapeDtypeStruct(shape, jnp.bfloat16) for shape in shapes),
        in_specs=[scalars] * 3 + [whole] * (3 + len(pieces) + len(others)),
        out_specs=tuple(whole for _ in shapes),
        scratch_shapes=[
            pltpu.VMEM((9, 3, len(pieces), each, channels), jnp.bfloat16),
            pltpu.VMEM((2, rows * per_row, 2 * width), jnp.float32),
            pltpu.VMEM((frames, positions, 2 * width), jnp.bfloat16),
        ],
        compiler_params=params(10),
        cost_estimate=pl.CostEstimate(
            flops=2 * rows * per_row * channels * width,
            bytes_accessed=2 * channels * width,
            transcendentals=0,
        ),
    )(places, slots, half, even, odd, bias, *pieces, *others)


def place_kernel(place_ref, *refs):
    *piece_refs, out_ref = refs
    width = piece_refs[0].shape[2]
    for p, piece_ref in enumerate(piece_refs):
        start = pl.multiple_of(place_ref[p] * width, LANES)
        out_ref[:, :, pl.ds(start, width)] = piece_ref[...]


def place(groups, pieces):
    held, positions, width = pieces[0].shape
    return pl.pallas_call(
        place_kernel,
        out_shape=jax.ShapeDtypeStruct((held, positions, width * len(pieces)), jnp.bfloat16),
        in_specs=[scalars] + [whole] * len(pieces),
        out_specs=whole,
        compiler_params=params(2),
    )(groups, *pieces)


def body(latents, norm_gain, norm_bias, conv_weight, conv_bias):
    held, row_count, col_count, channels = latents.shape
    group_count = lax.axis_size("frames")
    strips = lax.axis_size("rows")
    group = lax.axis_index("frames")
    strip = lax.axis_index("rows")
    is_line = strips == 4 * CORES
    weight = conv_weight.transpose(0, 1, 2, 4, 3)
    weight = weight.reshape((-1,) + weight.shape[3:])

    core = strip % CORES
    stats, inner, outer, payload = local(core[None], latents)
    sibling = lax.ppermute(inner, "rows", flip("rows", 1))
    facing = [(i, i + 1) for i in range(1, strips - 1, CORES)]
    facing = lax.ppermute(outer, "rows", facing + [(b, a) for a, b in facing])

    width = channels // group_count
    bias = lax.dynamic_slice_in_dim(conv_bias, group * width, width)[None]
    entries = held * row_count * col_count
    if is_line:
        weight = after(weight, sibling, facing)
        second = lax.ppermute(weight, "rows", flip("rows", 2 * CORES))
        for distance in (1, CORES, 2 * CORES):
            stats = merge([stats] + exchange(stats, "rows", [distance]), entries)
            entries *= 2
    else:
        distance = 1
        while distance < strips:
            stats = merge([stats] + exchange(stats, "rows", [distance]), entries)
            entries *= 2
            distance *= 2

    if is_line:
        last, second = lax.optimization_barrier((weight, second))
        second = hold(second)
        ends = chip_pairs([(1, 0), (2, 3)])
        middle = chip_pairs([(1, 2), (2, 1)])
        third_ends = lax.ppermute(second, "rows", ends)
        third_middle = lax.ppermute(last, "rows", middle)

    above = jnp.where(strip == 0, 2, 1 - core)
    below = jnp.where(strip == strips - 1, 2, core)
    edges = jnp.stack([above, below]).astype(jnp.int32)
    payload = pack(edges, stats, sibling, facing, payload, held, row_count + 2, col_count)
    if is_line:
        first = lax.ppermute(after(weight, payload), "rows", flip("rows", CORES))
    distances = [0] + list(reversed(range(1, group_count)))
    strip_pieces = [payload] + exchange(payload, "frames", distances[1:])
    groups = jnp.stack([group ^ d for d in range(group_count)]).astype(jnp.int32)
    affine = jnp.stack([norm_gain, norm_bias])
    if is_line:
        near, strip_pieces, far = lax.optimization_barrier(([weight, first], strip_pieces, [second]))
    places = jnp.stack([group ^ d for d in distances]).astype(jnp.int32) * held
    even, odd = activate(
        places, affine, strip_pieces, held, row_count + 2, col_count, entries
    )

    if is_line:
        near += [lax.ppermute(piece, "rows", flip("rows", 1)) for piece in near]
        slots = jnp.stack([strip, strip ^ 2, strip ^ 1, strip ^ 3]) % 4
        half, other_half = (strip // 4)[None], 1 - (strip // 4)[None]
    else:
        gathered = lax.all_gather(weight, "rows", axis=1, tiled=True)
        near, far = [gathered[:, : width // 2]], [gathered[:, width // 2 :]]
        slots = jnp.zeros((1,), jnp.int32)
        half, other_half = slots, slots + 1
    convolved = functools.partial(
        convolve, groups * held, slots, even=even, odd=odd, frames=held * group_count
    )
    done = convolved(half, bias=bias, pieces=near)[0]
    if is_line:
        third_ends, third_middle, done = lax.optimization_barrier((third_ends, third_middle, done))
        chip = strip // CORES
        at_end = ((chip == 0) | (chip == 3)).astype(jnp.int32)[None]
        third = pick(at_end, third_ends, third_middle)
        far.append(third)
        far += [lax.ppermute(piece, "rows", flip("rows", 1)) for piece in far]
    parts = convolved(other_half, bias=bias, pieces=far, other=done)
    parts = [parts[0]] + [
        lax.ppermute(parts[d], "frames", flip("frames", d)) for d in range(1, group_count)
    ]
    return place(groups, parts).reshape(latents.shape)


def solution(mesh):
    placed = (
        P("frames", "rows", None, None),
        P(),
        P(),
        P(None, None, None, None, ("frames", "rows")),
        P(),
    )
    return jax.shard_map(
        body, mesh=mesh, in_specs=placed, out_specs=P("frames", "rows", None, None), check_vma=False
    )
```

```python
import functools

import jax
import jax.numpy as jnp
from jax import lax
from jax.experimental import pallas as pl
from jax.experimental.pallas import tpu as pltpu
from jax.sharding import PartitionSpec as P

GROUPS = 32
LANES = 128
CORES = 2

epsilon = 1e-06

whole = pl.BlockSpec(memory_space=pltpu.VMEM)
scalars = pl.BlockSpec(memory_space=pltpu.SMEM)


def params(mib):
    return pltpu.CompilerParams(vmem_limit_bytes=mib * 2**20)


def flip(axis, distance):
    return [(i, i ^ distance) for i in range(lax.axis_size(axis))]


def exchange(block, axis, distances):
    return [lax.ppermute(block, axis, flip(axis, d)) for d in distances]


def chip_pairs(pairs):
    return [(CORES * a + c, CORES * b + c) for a, b in pairs for c in range(CORES)]


def after(block, *others):
    return lax.optimization_barrier((block, *others))[0]


def local_kernel(core_ref, x_ref, stats_ref, inner_ref, outer_ref, payload_ref):
    frames, rows, cols, channels = x_ref.shape
    entries = frames * rows * cols
    inner = (rows - 1) * (1 - core_ref[0])
    inner_ref[...] = x_ref[:, pl.ds(inner, 1)]
    outer_ref[...] = x_ref[:, pl.ds(rows - 1 - inner, 1)]
    for f in range(frames):
        start = (f * (rows + 2) + 1) * cols
        payload_ref[start : start + rows * cols, :] = x_ref[f].reshape(rows * cols, channels)
    for block in range(channels // LANES):
        lanes = pl.ds(block * LANES, LANES)
        total = jnp.zeros((8, LANES), jnp.float32)
        for f in range(frames):
            for r in range(rows):
                x = x_ref[f, r, :, lanes].astype(jnp.float32)
                total = total + jnp.sum(x.reshape(-1, 8, LANES), axis=0)
        mean = jnp.sum(total, axis=0, keepdims=True) / entries
        total = jnp.zeros((8, LANES), jnp.float32)
        for f in range(frames):
            for r in range(rows):
                x = x_ref[f, r, :, lanes].astype(jnp.float32) - mean
                total = total + jnp.sum((x * x).reshape(-1, 8, LANES), axis=0)
        stats_ref[0:1, lanes] = mean
        stats_ref[1:2, lanes] = jnp.sum(total, axis=0, keepdims=True)


def local(core, latents):
    frames, rows, cols, channels = latents.shape
    edge = jax.ShapeDtypeStruct((frames, 1, cols, channels), jnp.bfloat16)
    return pl.pallas_call(
        local_kernel,
        out_shape=(
            jax.ShapeDtypeStruct((2, channels), jnp.float32),
            edge,
            edge,
            jax.ShapeDtypeStruct((frames * (rows + 2) * cols + 16, channels), jnp.bfloat16),
        ),
        in_specs=[scalars, whole],
        out_specs=(whole,) * 4,
        compiler_params=params(2),
    )(core, latents)


def merge(parts, entries):
    mean = sum(part[0] for part in parts) / len(parts)
    apart = sum((part[0] - mean) ** 2 for part in parts) * entries
    return jnp.stack([mean, sum(part[1] for part in parts) + apart])


def pack_kernel(frames, rows, cols, edge_ref, stats_ref, sibling_ref, facing_ref, payload_ref, out_ref):
    count = frames * rows * cols
    out_ref[...] = payload_ref[...]
    for f in range(frames):
        first = f * rows * cols
        last = first + (rows - 1) * cols
        for start, edge, mirror in ((first, 0, first + 2 * cols), (last, 1, last - 2 * cols)):
            @pl.when(edge_ref[edge] == 0)
            def _():
                out_ref[start : start + cols, :] = sibling_ref[f, 0]

            @pl.when(edge_ref[edge] == 1)
            def _():
                out_ref[start : start + cols, :] = facing_ref[f, 0]

            @pl.when(edge_ref[edge] == 2)
            def _():
                out_ref[start : start + cols, :] = out_ref[mirror : mirror + cols, :]

    rest = stats_ref[...]
    terms = []
    for _ in range(3):
        term = rest.astype(jnp.bfloat16).astype(jnp.float32)
        terms.append(term)
        rest = rest - term
    unused = out_ref.shape[0] - count - 6
    terms.append(jnp.zeros((unused, rest.shape[1]), jnp.float32))
    out_ref[count:, :] = jnp.concatenate(terms, axis=0).astype(jnp.bfloat16)


def pack(edges, stats, sibling, facing, payload, frames, rows, cols):
    return pl.pallas_call(
        functools.partial(pack_kernel, frames, rows, cols),
        out_shape=jax.ShapeDtypeStruct(payload.shape, jnp.bfloat16),
        in_specs=[scalars] + [whole] * 4,
        out_specs=whole,
        compiler_params=params(2),
    )(edges, stats, sibling, facing, payload)


def held_kernel(in_ref, out_ref):
    out_ref[...] = in_ref[...]


def hold(block):
    return pl.pallas_call(
        held_kernel,
        out_shape=jax.ShapeDtypeStruct(block.shape, block.dtype),
        in_specs=[whole],
        out_specs=whole,
        compiler_params=params(1),
        cost_estimate=pl.CostEstimate(flops=10**10, bytes_accessed=0, transcendentals=0),
    )(block)


def pick_kernel(which_ref, one_ref, other_ref, out_ref):
    @pl.when(which_ref[0] != 0)
    def _():
        out_ref[...] = one_ref[...]

    @pl.when(which_ref[0] == 0)
    def _():
        out_ref[...] = other_ref[...]


def pick(which, one, other):
    return pl.pallas_call(
        pick_kernel,
        out_shape=jax.ShapeDtypeStruct(one.shape, one.dtype),
        in_specs=[scalars] + [whole] * 2,
        out_specs=whole,
        compiler_params=params(2),
        cost_estimate=pl.CostEstimate(flops=0, bytes_accessed=one.size, transcendentals=0),
    )(which, one, other)


def lane_group_sum(x, size):
    lane = lax.broadcasted_iota(jnp.int32, x.shape, 1)
    step = 1
    while step < size:
        up = pltpu.roll(x, x.shape[1] - step, 1)
        down = pltpu.roll(x, step, 1)
        x = x + jnp.where((lane & step) == 0, up, down)
        step *= 2
    return x


def activate_kernel(held, rows, entries, place_ref, affine_ref, *refs):
    *piece_refs, even_ref, odd_ref, scratch, norm = refs
    channels = piece_refs[0].shape[1]
    frames = held * len(piece_refs)
    cols = odd_ref.shape[1] // frames
    tail = held * rows * cols
    size = channels // GROUPS

    def norms(lanes):
        means, squares = [], []
        for piece_ref in piece_refs:
            terms = piece_ref[tail : tail + 16, lanes].astype(jnp.float32)
            both = terms[0:2] + terms[2:4] + terms[4:6]
            means.append(both[0:1])
            squares.append(both[1:2])
        count = len(piece_refs) * size
        mean = lane_group_sum(jnp.broadcast_to(sum(means), (8, LANES)), size) / count
        spread = sum(squares) + entries * sum((m - mean[0:1]) ** 2 for m in means)
        var = lane_group_sum(jnp.broadcast_to(spread, (8, LANES)), size) / (count * entries)
        norm[0:1, lanes] = mean[0:1]
        norm[1:2, lanes] = lax.rsqrt(var[0:1] + epsilon) * affine_ref[0:1, lanes]
        norm[2:3, lanes] = affine_ref[1:2, lanes]

    blocks = channels // LANES
    for block in range(blocks):
        norms(pl.ds(block * LANES, LANES))
    last = (cols + 1) * frames

    def step(index, carry):
        pair, block = index // blocks, index % blocks
        lanes = pl.ds(pl.multiple_of(block * LANES, LANES), LANES)
        mean, scale, bias = norm[0:1, lanes], norm[1:2, lanes], norm[2:3, lanes]
        for p, piece_ref in enumerate(piece_refs):
            for f in range(held):
                start = pl.multiple_of((f * rows + 2 * pair) * cols, 16)
                x = piece_ref[pl.ds(start, 2 * cols), lanes].astype(jnp.float32)
                h = 0.5 * ((x - mean) * scale + bias)
                h = h + h * jnp.tanh(h)
                for r in range(2):
                    scratch[r, pl.ds(frames + place_ref[p] + f, cols, stride=frames), :] = h[r * cols : (r + 1) * cols]
        for r in range(2):
            scratch[r, 0:frames, :] = scratch[r, 2 * frames : 3 * frames, :]
            scratch[r, last : last + frames, :] = scratch[r, last - 2 * frames : last - frames, :]
            even_ref[2 * pair + r, :, lanes] = scratch[r].astype(jnp.bfloat16)
            odd_ref[2 * pair + r, :, lanes] = scratch[r, frames:last, :].astype(jnp.bfloat16)
        return carry

    lax.fori_loop(0, rows // 2 * blocks, step, 0)


def activate(places, affine, pieces, held, rows, cols, entries):
    channels = pieces[0].shape[1]
    frames = held * len(pieces)
    return pl.pallas_call(
        functools.partial(activate_kernel, held, rows, entries),
        out_shape=(
            jax.ShapeDtypeStruct((rows, (cols + 2) * frames, channels), jnp.bfloat16),
            jax.ShapeDtypeStruct((rows, cols * frames, channels), jnp.bfloat16),
        ),
        in_specs=[scalars, whole] + [whole] * len(pieces),
        out_specs=(whole, whole),
        scratch_shapes=[
            pltpu.VMEM((2, (cols + 2) * frames, LANES), jnp.float32),
            pltpu.VMEM((3, channels), jnp.float32),
        ],
        compiler_params=params(4),
        cost_estimate=pl.CostEstimate(
            flops=10 * frames * rows * cols * channels,
            bytes_accessed=6 * frames * rows * cols * channels,
            transcendentals=frames * rows * cols * channels,
        ),
    )(places, affine, *pieces)


def conv_kernel(count, with_other, place_ref, slot_ref, half_ref, even_ref, odd_ref, bias_ref, *refs):
    piece_refs, refs = refs[:count], refs[count:]
    if with_other:
        other_ref, refs = refs[0], refs[1:]
    out_refs, (taps, sums, placed) = refs[:-3], refs[-3:]
    rows = even_ref.shape[0] - 2
    per_row = odd_ref.shape[1]
    frames = placed.shape[0]
    cols = per_row // frames
    channels = even_ref.shape[2]
    width = taps.shape[2] * taps.shape[3]
    for p, piece_ref in enumerate(piece_refs):
        slot = slot_ref[p]
        for tap in range(27):
            taps[tap % 9, tap // 9, slot] = piece_ref[tap]

    for y in range(rows):
        total = None
        for tap in range(9):
            b, c = tap // 3, tap % 3
            if c == 1:
                window = odd_ref[y + b]
            else:
                window = even_ref[y + b, pl.ds(c * frames, per_row), :]
            product = lax.dot_general(
                window,
                taps[tap].reshape(3 * width, channels),
                (((1,), (1,)), ((), ())),
                preferred_element_type=jnp.float32,
            )
            total = product if total is None else total + product
        place = slice(y * per_row, (y + 1) * per_row)
        sums[0, place, :] = total[:, : 2 * width]
        sums[1, place, 0:width] = total[:, 2 * width :]

    count = rows * cols
    lane = lax.broadcasted_iota(jnp.int32, (count, 2 * width), 1)
    low = lane < width
    for f in range(frames):
        value = sums[1, pl.ds(f, count, stride=frames), :]
        if f >= 1:
            value = value + pltpu.roll(sums[0, pl.ds(f - 1, count, stride=frames), :], width, 1)
        if f >= 2:
            value = value + sums[0, pl.ds(f - 2, count, stride=frames), :]
        value = jnp.where(low, value, pltpu.roll(value, width, 1)) + bias_ref[...]
        if with_other:
            value = jnp.where(low == (half_ref[0] == 0), value, other_ref[f].astype(jnp.float32))
        placed[f] = value.astype(jnp.bfloat16)
    if with_other:
        for p, out_ref in enumerate(out_refs):
            out_ref[...] = placed[pl.ds(place_ref[p], out_ref.shape[0])]
    else:
        out_refs[0][...] = placed[...]


def convolve(places, slots, half, even, odd, bias, pieces, frames, other=None):
    rows, per_row, channels = even.shape[0] - 2, odd.shape[1], even.shape[2]
    positions = rows * per_row // frames
    each = pieces[0].shape[1]
    width = each * len(pieces)
    if other is None:
        shapes, others = [(frames, positions, 2 * width)], []
    else:
        groups = places.shape[0]
        shapes, others = [(frames // groups, positions, 2 * width)] * groups, [other]
    return pl.pallas_call(
        functools.partial(conv_kernel, len(pieces), other is not None),
        out_shape=tuple(jax.ShapeDtypeStruct(shape, jnp.bfloat16) for shape in shapes),
        in_specs=[scalars] * 3 + [whole] * (3 + len(pieces) + len(others)),
        out_specs=tuple(whole for _ in shapes),
        scratch_shapes=[
            pltpu.VMEM((9, 3, len(pieces), each, channels), jnp.bfloat16),
            pltpu.VMEM((2, rows * per_row, 2 * width), jnp.float32),
            pltpu.VMEM((frames, positions, 2 * width), jnp.bfloat16),
        ],
        compiler_params=params(10),
        cost_estimate=pl.CostEstimate(
            flops=2 * rows * per_row * channels * width,
            bytes_accessed=2 * channels * width,
            transcendentals=0,
        ),
    )(places, slots, half, even, odd, bias, *pieces, *others)


def place_kernel(place_ref, *refs):
    *piece_refs, out_ref = refs
    width = piece_refs[0].shape[2]
    for p, piece_ref in enumerate(piece_refs):
        start = pl.multiple_of(place_ref[p] * width, LANES)
        out_ref[:, :, pl.ds(start, width)] = piece_ref[...]


def place(groups, pieces):
    held, positions, width = pieces[0].shape
    return pl.pallas_call(
        place_kernel,
        out_shape=jax.ShapeDtypeStruct((held, positions, width * len(pieces)), jnp.bfloat16),
        in_specs=[scalars] + [whole] * len(pieces),
        out_specs=whole,
        compiler_params=params(2),
    )(groups, *pieces)


def body(latents, norm_gain, norm_bias, conv_weight, conv_bias):
    held, row_count, col_count, channels = latents.shape
    group_count = lax.axis_size("frames")
    strips = lax.axis_size("rows")
    group = lax.axis_index("frames")
    strip = lax.axis_index("rows")
    is_line = strips == 4 * CORES
    weight = conv_weight.transpose(0, 1, 2, 4, 3)
    weight = weight.reshape((-1,) + weight.shape[3:])

    core = strip % CORES
    stats, inner, outer, payload = local(core[None], latents)
    sibling = lax.ppermute(inner, "rows", flip("rows", 1))
    facing = [(i, i + 1) for i in range(1, strips - 1, CORES)]
    facing = lax.ppermute(outer, "rows", facing + [(b, a) for a, b in facing])

    width = channels // group_count
    bias = lax.dynamic_slice_in_dim(conv_bias, group * width, width)[None]
    entries = held * row_count * col_count
    if is_line:
        weight = after(weight, sibling, facing)
        second = lax.ppermute(weight, "rows", flip("rows", 2 * CORES))
        for distance in (1, CORES, 2 * CORES):
            stats = merge([stats] + exchange(stats, "rows", [distance]), entries)
            entries *= 2
    else:
        distance = 1
        while distance < strips:
            stats = merge([stats] + exchange(stats, "rows", [distance]), entries)
            entries *= 2
            distance *= 2

    if is_line:
        last, second = lax.optimization_barrier((weight, second))
        second = hold(second)
        ends = chip_pairs([(1, 0), (2, 3)])
        middle = chip_pairs([(1, 2), (2, 1)])
        third_ends = lax.ppermute(second, "rows", ends)
        third_middle = lax.ppermute(last, "rows", middle)

    above = jnp.where(strip == 0, 2, 1 - core)
    below = jnp.where(strip == strips - 1, 2, core)
    edges = jnp.stack([above, below]).astype(jnp.int32)
    payload = pack(edges, stats, sibling, facing, payload, held, row_count + 2, col_count)
    if is_line:
        first = lax.ppermute(after(weight, payload), "rows", flip("rows", CORES))
    distances = [0] + list(reversed(range(1, group_count)))
    strip_pieces = [payload] + exchange(payload, "frames", distances[1:])
    groups = jnp.stack([group ^ d for d in range(group_count)]).astype(jnp.int32)
    affine = jnp.stack([norm_gain, norm_bias])
    if is_line:
        near, strip_pieces, far = lax.optimization_barrier(([weight, first], strip_pieces, [second]))
    places = jnp.stack([group ^ d for d in distances]).astype(jnp.int32) * held
    even, odd = activate(
        places, affine, strip_pieces, held, row_count + 2, col_count, entries
    )

    if is_line:
        near += [lax.ppermute(piece, "rows", flip("rows", 1)) for piece in near]
        slots = jnp.stack([strip, strip ^ 2, strip ^ 1, strip ^ 3]) % 4
        half, other_half = (strip // 4)[None], 1 - (strip // 4)[None]
    else:
        gathered = lax.all_gather(weight, "rows", axis=1, tiled=True)
        near, far = [gathered[:, : width // 2]], [gathered[:, width // 2 :]]
        slots = jnp.zeros((1,), jnp.int32)
        half, other_half = slots, slots + 1
    convolved = functools.partial(
        convolve, groups * held, slots, even=even, odd=odd, frames=held * group_count
    )
    done = convolved(half, bias=bias, pieces=near)[0]
    if is_line:
        third_ends, third_middle, done = lax.optimization_barrier((third_ends, third_middle, done))
        chip = strip // CORES
        at_end = ((chip == 0) | (chip == 3)).astype(jnp.int32)[None]
        third = pick(at_end, third_ends, third_middle)
        far.append(third)
        far += [lax.ppermute(piece, "rows", flip("rows", 1)) for piece in far]
    parts = convolved(other_half, bias=bias, pieces=far, other=done)
    parts = [parts[0]] + [
        lax.ppermute(parts[d], "frames", flip("frames", d)) for d in range(1, group_count)
    ]
    return place(groups, parts).reshape(latents.shape)


def solution(mesh):
    placed = (
        P("frames", "rows", None, None),
        P(),
        P(),
        P(None, None, None, None, ("frames", "rows")),
        P(),
    )
    return jax.shard_map(
        body, mesh=mesh, in_specs=placed, out_specs=P("frames", "rows", None, None), check_vma=False
    )
```
